256 devices in a mesh: space: 64 (over x, z_hi, y), batch: 4 (over z_lo, core).
Axes of the slice: x: 4, y: 4, z: 8 (z_hi: 4, z_lo: 2; z = z_hi * 2 + z_lo), core: 2. Of those that a mesh axis runs over, the one named last changes fastest.
Arguments:
- volumes: bfloat16 [8, 4, 256, 16, 256], P('batch', None, 'space'), may hold values from -6 to 6
- first_kernel: bfloat16 [16, 4, 3, 3, 3], replicated, may hold values from -0.625 to 0.625
- second_kernel: bfloat16 [32, 16, 3, 3, 3], replicated, may hold values from -0.875 to 0.875
- cotangent: bfloat16 [8, 32, 128, 8, 128], P('batch', None, 'space'), may hold values from -6 to 6
Outputs:
- activation: bfloat16 [8, 32, 128, 8, 128], P('batch', None, 'space')
- pooled_grad: bfloat16 [8, 16, 128, 8, 128], P('batch', None, 'space')
- first_grad: float32 [16, 4, 3, 3, 3], replicated
- second_grad: float32 [32, 16, 3, 3, 3], replicated
The draws below stay inside these ranges and needn't reach their ends.
All inputs are finite; a program needn't handle non-finite values.
Results may differ from the reference program's by a relative error of at most 0.0057.
Values may be sent and summed in bfloat16 or wider, within the bound.
A program may use at most 192 MiB of HBM per device.

```python
import math
import jax
import jax.numpy as jnp
from jax import lax

C0 = 4
C1 = 16
C2 = 32
NY = 16
NZ = 256
BATCH = 8
NX = 256


def shard_levels(key, shape, split, low, high):
    gain = 1.0
    for dim, parts in split:
        steps = jax.random.uniform(jax.random.fold_in(jax.random.fold_in(key, 6), dim), (parts,), jnp.float32, low / len(split), high / len(split))
        gain = gain * jnp.repeat(jnp.exp(steps), shape[dim] // parts).reshape((-1,) + (1,) * (len(shape) - 1 - dim))
    return gain


def gaussian(own_key, dims, scale, reach, shards=(), kind=jnp.bfloat16):
    loudness = shard_levels(own_key, dims, shards, -0.22, 0.18) if shards else 1.0
    array = jax.random.normal(own_key, dims, jnp.float32) * scale * loudness
    return jnp.minimum(jnp.maximum(array, -reach), reach).astype(kind)


def setup_inputs(seed: int = 0) -> dict:
    key_list = jax.random.split(jax.random.key(seed), 5)
    volumes = gaussian(key_list[0], (BATCH, C0, NX, NY, NZ), 1.0, 6.0, ((0, 4), (2, 64)))
    first_kernel = gaussian(key_list[1], (C1, C0, 3, 3, 3), (27 * C0) ** -0.5, 0.625)
    second_kernel = gaussian(key_list[2], (C2, C1, 3, 3, 3), 54 ** -0.5, 0.875)
    cotangent = gaussian(key_list[3], (BATCH, C2, NX // 2, NY // 2, NZ // 2), 1.0, 6.0, ((0, 4), (2, 64)))
    return dict(volumes=volumes, first_kernel=first_kernel, second_kernel=second_kernel, cotangent=cotangent)


layout = ('NCDHW', 'OIDHW', 'NCDHW')
swapped = ('CNDHW', 'IODHW', 'CNDHW')

def convolve(field, kernel):
    return lax.conv_general_dilated(field, kernel, (1, 1, 1), ((1, 1), (1, 1), (1, 1)), dimension_numbers=layout, preferred_element_type=jnp.float32)

def kernel_grad(field, gradient):
    return lax.conv_general_dilated(field, gradient, (1, 1, 1), ((1, 1), (1, 1), (1, 1)), dimension_numbers=swapped, preferred_element_type=jnp.float32)

def transposed(kernel):
    return jnp.transpose(jnp.flip(kernel, (2, 3, 4)), (1, 0, 2, 3, 4))

def smooth_unit(values):
    return 0.3 * values + 0.7 * values * jax.nn.sigmoid(values)

def unit_slope(values):
    squash = jax.nn.sigmoid(values)
    return 0.3 + 0.7 * (squash + values * squash * (1.0 - squash))

def average_pool(field):
    shape = field.shape
    blocks = field.reshape(shape[0], shape[1], shape[2] // 2, 2, shape[3] // 2, 2, shape[4] // 2, 2)
    return lax.optimization_barrier(jnp.mean(blocks, axis=(3, 5, 7)))

def spread(gradient):
    shape = gradient.shape
    grown = jnp.broadcast_to(gradient[:, :, :, None, :, None, :, None], (shape[0], shape[1], shape[2], 2, shape[3], 2, shape[4], 2))
    return grown.reshape(shape[0], shape[1], 2 * shape[2], 2 * shape[3], 2 * shape[4])

def reference(volumes, first_kernel, second_kernel, cotangent):

    def one_sample(paired):
        volume = paired[0][None]
        upstream = paired[1][None]
        first_pre = convolve(volume, first_kernel)
        pooled = average_pool(smooth_unit(first_pre)).astype(jnp.bfloat16)
        second_pre = convolve(pooled, second_kernel)
        activation = smooth_unit(second_pre).astype(jnp.bfloat16)
        second_delta = (upstream * unit_slope(second_pre)).astype(jnp.bfloat16)
        backward = convolve(second_delta, transposed(second_kernel))
        first_delta = (spread(backward) * 0.125 * unit_slope(first_pre)).astype(jnp.bfloat16)
        return (activation[0], backward.astype(jnp.bfloat16)[0], kernel_grad(volume, first_delta), kernel_grad(pooled, second_delta))
    activation, pooled_grad, first_terms, second_terms = lax.map(one_sample, (volumes, cotangent))
    cells = BATCH * NX * NY * NZ
    first_grad = lax.optimization_barrier(jnp.sum(first_terms, axis=0)) * (1.0 / math.sqrt(cells))
    second_grad = lax.optimization_barrier(jnp.sum(second_terms, axis=0)) * (1.0 / math.sqrt(cells / 8))
    return (activation, pooled_grad, first_grad, second_grad)
```

```python
import functools
import math

import jax
import jax.numpy as jnp
from jax import lax
from jax.experimental import pallas as pl
from jax.experimental.pallas import tpu as pltpu
from jax.sharding import PartitionSpec as P

F32 = jnp.float32
BF16 = jnp.bfloat16
MESH = pl.DeviceIdType.MESH


def space_grid(count):
    side = round(count ** (1 / 3))
    if side**3 == count:
        return side, side, side
    return 2, 1, count // 2


def dot(a, b):
    return jnp.dot(a, b, preferred_element_type=F32)


def dot_nt(a, b):
    return lax.dot_general(a, b, (((1,), (1,)), ((), ())), preferred_element_type=F32)


def shifts(v):
    lanes = lax.broadcasted_iota(jnp.int32, v.shape, 1)
    width = v.shape[1]
    before = jnp.where(lanes == 0, 0.0, pltpu.roll(v, 1, 1))
    after = jnp.where(lanes == width - 1, 0.0, pltpu.roll(v, width - 1, 1))
    return before, after


def split(v):
    high = v.astype(BF16)
    return high, (v - high.astype(F32)).astype(BF16)


def act_and_slope(z):
    t = jnp.tanh(0.5 * z)
    a = 0.65 + 0.35 * t
    return z * a, a + (0.175 * z) * (1.0 - t * t)


def kernel(
    sizes, scales, vol, w1, w2, cot, out_act, out_pg, out_g1, out_g2,
    vbuf, vf, u1, slope, pb, ph, u2, cotb, cotf, actf, actb, db, dh, u3, bkf, bkb,
    a1s, a2s, w2f, a1, a2, a3, acc1, acc2, pack, r1, r2, res, flat,
    local_sem, halo_send, halo_recv, sum_send, sum_recv,
):
    (nx, nzh, ny), nb = sizes
    n_space = nx * nzh * ny
    g1, g2 = nx * ny, nzh * nb
    tp = 16 // g1
    sp, bt = lax.axis_index("space"), lax.axis_index("batch")
    xi = lax.div(sp, nzh * ny)
    zi = lax.rem(lax.div(sp, ny), nzh)
    yi = lax.rem(sp, ny)
    i1 = xi * ny + yi
    i2 = zi * nb + bt
    right = lax.rem(sp + 1, n_space)
    left = lax.rem(sp + n_space - 1, n_space)

    def peer1(p):
        return (lax.div(p, ny) * (nzh * ny) + zi * ny + lax.rem(p, ny), bt)

    def peer2(p):
        return (xi * (nzh * ny) + lax.div(p, nb) * ny + yi, lax.rem(p, nb))

    barrier = pltpu.get_barrier_semaphore()
    for side in (left, right):
        pl.semaphore_signal(barrier, inc=1, device_id=(side, bt), device_id_type=MESH)

    def greet1(d, c):
        pl.semaphore_signal(barrier, inc=1, device_id=peer1(lax.rem(i1 + d, g1)), device_id_type=MESH)
        return c

    def greet2(d, c):
        pl.semaphore_signal(barrier, inc=1, device_id=peer2(lax.rem(i2 + d, g2)), device_id_type=MESH)
        return c

    lax.fori_loop(1, g1, greet1, 0)
    lax.fori_loop(1, g2, greet2, 0)

    own = []
    for s in range(2):
        for x in range(4):
            own.append(pltpu.make_async_copy(vol.at[s, :, x], vbuf.at[s, x + 1], local_sem.at[s * 4 + x]))
    own.append(pltpu.make_async_copy(cot, cotb, local_sem.at[8]))
    for c in own:
        c.start()

    pl.semaphore_wait(barrier, 2 + g1 - 1 + g2 - 1)

    def both_ways(k, to_right, land_right, to_left, land_left):
        one = pltpu.make_async_remote_copy(
            src_ref=to_right, dst_ref=land_right, send_sem=halo_send.at[k, 0], recv_sem=halo_recv.at[k, 0],
            device_id=(right, bt), device_id_type=MESH,
        )
        two = pltpu.make_async_remote_copy(
            src_ref=to_left, dst_ref=land_left, send_sem=halo_send.at[k, 1], recv_sem=halo_recv.at[k, 1],
            device_id=(left, bt), device_id_type=MESH,
        )
        return one, two

    halos = [both_ways(s, vol.at[s, :, 3], vbuf.at[s, 0], vol.at[s, :, 0], vbuf.at[s, 5]) for s in range(2)]
    for pair in halos:
        for c in pair:
            c.start()

    def arrive(pair, low, high):
        for c in pair:
            c.wait()

        @pl.when(sp == 0)
        def _():
            low[...] = jnp.zeros_like(low)

        @pl.when(sp == n_space - 1)
        def _():
            high[...] = jnp.zeros_like(high)

    a1s[...] = jnp.zeros_like(a1s)
    for kx in range(3):
        for ky in range(3):
            for kz in range(3):
                row = ky * 80 + kz * 24 + kx * 4
                a1s[row : row + 4, 0:16] = w1[kx, ky, kz].astype(F32)
    base = a1s[...]
    t1 = base
    for x in range(1, 4):
        t1 = t1 + pltpu.roll(pltpu.roll(base, 4 * x, 0), 16 * x, 1)
    a1[...] = t1.T[0:64].astype(BF16)

    w2f[...] = jnp.zeros_like(w2f)
    w2f[:, 0:32] = w2[...].reshape(432, 32).astype(F32)
    a2s[...] = jnp.zeros_like(a2s)
    for ky in range(3):
        for kx in range(3):
            a2s[ky * 192 + kx * 48 : ky * 192 + kx * 48 + 48, :] = w2f[(kx * 3 + ky) * 48 : (kx * 3 + ky) * 48 + 48, :]
    base = a2s[...]
    t2 = base + pltpu.roll(pltpu.roll(base, 48, 0), 32, 1)
    a2[...] = t2.T[0:64].astype(BF16)
    for ky in range(3):
        for kz in range(3):
            rows = [((kx * 3 + 2 - ky) * 3 + 2 - kz) * 16 for kx in range(3)]
            blocks = [w2f[r : r + 16, :] for r in rows]
            first = blocks[2] + pltpu.roll(blocks[1], 32, 1) + pltpu.roll(blocks[0], 64, 1)
            both = jnp.concatenate([first, pltpu.roll(first, 32, 1)], axis=0)
            a3[:, (ky * 3 + kz) * 128 : (ky * 3 + kz) * 128 + 128] = both.astype(BF16)

    zrow = lax.broadcasted_iota(jnp.int32, (256, 128), 0)
    zcol = lax.broadcasted_iota(jnp.int32, (256, 128), 1)
    halve = jnp.where(lax.div(zrow, 2) == zcol, 0.125, 0.0).astype(BF16)
    zrow = lax.broadcasted_iota(jnp.int32, (128, 256), 0)
    zcol = lax.broadcasted_iota(jnp.int32, (128, 256), 1)
    double = jnp.where(zrow == lax.div(zcol, 2), 1.0, 0.0).astype(BF16)

    acc1[...] = jnp.zeros_like(acc1)
    acc2[...] = jnp.zeros_like(acc2)
    for s in range(2):
        u1[s, 0:80, :] = jnp.zeros((80, 256), BF16)
        u1[s, 1360:1456, :] = jnp.zeros((96, 256), BF16)
        u2[s, 0:192, :] = jnp.zeros((192, 128), BF16)
        u2[s, 1728:1984, :] = jnp.zeros((256, 128), BF16)
        u3[s, 0:384, :] = jnp.zeros((384, 128), BF16)
        u3[s, 3456:3840, :] = jnp.zeros((384, 128), BF16)

    def stage1(s):
        for c in own[s * 4 : s * 4 + 4]:
            c.wait()
        arrive(halos[s], vbuf.at[s, 0], vbuf.at[s, 5])
        planes = vbuf[s].reshape(384, 256).astype(F32)
        for half in range(2):
            vf[half] = planes[:, 128 * half : 128 * half + 128]

        def fill(y, c):
            v = jnp.concatenate([vf[half, pl.ds(y, 24, stride=16), :] for half in range(2)], axis=1)
            before, after = shifts(v)
            rows = jnp.concatenate([before, v, after, jnp.zeros((8, 256), F32)], axis=0)
            u1[s, pl.ds(pl.multiple_of((y + 1) * 80, 16), 80), :] = rows.astype(BF16)
            return c

        lax.fori_loop(0, 16, fill, 0, unroll=4)

        def forward(j, c):
            total = None
            for i in range(2):
                y = 2 * j + i
                pre = dot(a1[...], u1[s, pl.ds(pl.multiple_of(y * 80, 16), 256), :])
                act, sl = act_and_slope(pre)
                slope[s, pl.ds(pl.multiple_of(y * 64, 64), 64), :] = 0.125 * sl
                total = act if total is None else total + act
            pairs = jnp.concatenate([total[0:16] + total[16:32], total[32:48] + total[48:64]], axis=0)
            high, low = split(pairs)
            pooled = (dot(high, halve) + dot(low, halve)).astype(BF16)
            pb[s, j] = pooled.reshape(2, 16, 128)
            mid = pooled.astype(F32)
            before, after = shifts(mid)
            for x in range(2):
                part = slice(16 * x, 16 * x + 16)
                rows = jnp.concatenate([before[part], mid[part], after[part]], axis=0)
                u2[s, pl.ds(pl.multiple_of((j + 1) * 192 + (x + 1) * 48, 16), 48), :] = rows.astype(BF16)
            return c

        lax.fori_loop(0, 8, forward, 0, unroll=4)
        pair = both_ways(2 + s, pb.at[s, :, 1], ph.at[s, 0], pb.at[s, :, 0], ph.at[s, 1])
        for c in pair:
            c.start()
        return pair

    def stage2(s, pair):
        if s == 0:
            own[8].wait()
        cotf[...] = cotb[s].reshape(512, 128).astype(F32)
        arrive(pair, ph.at[s, 0], ph.at[s, 1])

        def fill(j, c):
            for side in range(2):
                mid = ph[s, side, j].astype(F32)
                before, after = shifts(mid)
                rows = jnp.concatenate([before, mid, after], axis=0)
                u2[s, pl.ds(pl.multiple_of((j + 1) * 192 + side * 144, 16), 48), :] = rows.astype(BF16)
            return c

        lax.fori_loop(0, 8, fill, 0, unroll=4)

        def forward(j, c):
            pre = dot(a2[...], u2[s, pl.ds(pl.multiple_of(j * 192, 64), 640), :])
            act, sl = act_and_slope(pre)
            got = []
            for x in range(2):
                actf[pl.ds(x * 8 + j, 32, stride=16), :] = act[32 * x : 32 * x + 32]
                got.append(cotf[pl.ds(x * 8 + j, 32, stride=16), :])
            delta = (jnp.concatenate(got, axis=0) * sl).astype(BF16)
            db[s, j] = delta.reshape(2, 32, 128)
            mid = delta.astype(F32)
            before, after = shifts(mid)
            for kz, rows in enumerate((before, mid, after)):
                u3[s, pl.ds(pl.multiple_of((j + 1) * 384 + kz * 128 + 32, 32), 64), :] = rows.astype(BF16)
            return c

        lax.fori_loop(0, 8, forward, 0, unroll=4)
        out = both_ways(4 + s, db.at[s, :, 1], dh.at[s, 0], db.at[s, :, 0], dh.at[s, 1])
        for c in out:
            c.start()
        actb[s] = actf[...].reshape(32, 2, 8, 128).astype(BF16)
        act_copy = pltpu.make_async_copy(actb.at[s], out_act.at[s], local_sem.at[9 + s])
        act_copy.start()

        def grad(j, c):
            field = jnp.concatenate(
                [u2[s, pl.ds(pl.multiple_of((2 * j + i) * 192, 64), 576), :] for i in range(2)], axis=1
            )
            delta = jnp.concatenate([db[s, 2 * j + i].reshape(64, 128) for i in range(2)], axis=1)
            acc2[:, 0:64] += dot_nt(field, delta)
            return c

        lax.fori_loop(0, 4, grad, 0, unroll=2)
        return out, act_copy

    def stage3(s, pair):
        arrive(pair, dh.at[s, 0], dh.at[s, 1])

        def fill(j, c):
            for side in range(2):
                mid = dh[s, side, j].astype(F32)
                before, after = shifts(mid)
                for kz, rows in enumerate((before, mid, after)):
                    at = pl.multiple_of((j + 1) * 384 + kz * 128 + side * 96, 32)
                    u3[s, pl.ds(at, 32), :] = rows.astype(BF16)
            return c

        lax.fori_loop(0, 8, fill, 0, unroll=4)

        def backward(j, c):
            back = dot(a3[...], u3[s, pl.ds(pl.multiple_of(j * 384, 128), 1152), :])
            for x in range(2):
                bkf[pl.ds(x * 8 + j, 16, stride=16), :] = back[16 * x : 16 * x + 16]
            high, low = split(back)
            up = dot(high, double) + dot(low, double)
            up = jnp.concatenate([up[0:16], up[0:16], up[16:32], up[16:32]], axis=0)
            fields, deltas = [], []
            for i in range(2):
                y = 2 * j + i
                deltas.append((up * slope[s, pl.ds(pl.multiple_of(y * 64, 64), 64), :]).astype(BF16))
                fields.append(u1[s, pl.ds(pl.multiple_of(y * 80, 16), 256), :])
            acc1[:, 0:64] += dot_nt(jnp.concatenate(fields, axis=1), jnp.concatenate(deltas, axis=1))
            return c

        lax.fori_loop(0, 8, backward, 0, unroll=4)
        bkb[s] = bkf[...].reshape(16, 2, 8, 128).astype(BF16)
        copy = pltpu.make_async_copy(bkb.at[s], out_pg.at[s], local_sem.at[11 + s])
        copy.start()
        return copy

    pooled_pairs = [stage1(0), stage1(1)]
    second = [stage2(s, pooled_pairs[s]) for s in range(2)]
    third = [stage3(s, second[s][0]) for s in range(2)]

    lanes = lax.broadcasted_iota(jnp.int32, (432, 128), 1)
    g = acc2[...].reshape(3, 192, 128)
    upper = g[:, 48:192].reshape(432, 128)
    f2 = jnp.where(lanes < 32, g[:, 0:144].reshape(432, 128) + pltpu.roll(upper, 96, 1), 0.0)
    g = acc1[0:240, :]
    f1 = g
    for x in range(1, 4):
        f1 = f1 + pltpu.roll(pltpu.roll(g, 240 - 4 * x, 0), 128 - 16 * x, 1)
    rows = lax.rem(lax.broadcasted_iota(jnp.int32, (240, 128), 0), 80)
    f1 = jnp.where(lax.broadcasted_iota(jnp.int32, (240, 128), 1) < 16, f1, 0.0)
    f1c = None
    for kz in range(3):
        part = jnp.where((rows >= 24 * kz) & (rows < 24 * kz + 12), f1, 0.0)
        part = pltpu.roll(part, 240 - 12 * kz, 0) if kz else part
        f1c = part if f1c is None else f1c + part
    f1c = f1c.reshape(3, 80, 128)[:, 0:40].reshape(120, 128)
    f1c = jnp.concatenate([f1c, jnp.zeros((8, 128), F32)], axis=0)
    body = pltpu.roll(f1c, 96, 1)
    rest = []
    for ky in range(3):
        part = f2[ky * 144 : ky * 144 + 128]
        body = body + (pltpu.roll(part, 32 * ky, 1) if ky else part)
        rest.append(f2[ky * 144 + 128 : ky * 144 + 144])
    rest = jnp.concatenate(rest, axis=0)
    lanes = lanes[0:48]
    first = jnp.where(lanes < 16, rest, 0.0)
    last = jnp.where(lanes >= 16, rest, 0.0)
    extra = jnp.concatenate([pltpu.roll(first, 112, 1), pltpu.roll(last, 96, 1), jnp.zeros((32, 128), F32)], axis=0)
    pack[...] = (body + extra).reshape(16, 8, 128)

    def spread_out(phase, group, index, peer, src, dst):
        def make(d):
            other = lax.rem(index + d, group)
            return pltpu.make_async_remote_copy(
                src_ref=src(other), dst_ref=dst, send_sem=sum_send.at[phase, d], recv_sem=sum_recv.at[phase, d],
                device_id=peer(other), device_id_type=MESH,
            )

        def go(d, c):
            make(d).start()
            return c

        def end(d, c):
            make(d).wait()
            return c

        lax.fori_loop(1, group, go, 0)
        lax.fori_loop(1, group, end, 0)

    mine = pl.ds(i1 * tp, tp)
    r1[i1] = pack[mine]
    spread_out(0, g1, i1, peer1, lambda p: pack.at[pl.ds(p * tp, tp)], r1.at[i1])
    r2[i2] = jnp.sum(r1[...], axis=0)
    spread_out(1, g2, i2, peer2, lambda p: r2.at[i2], r2.at[i2])
    res[i1] = jnp.sum(r2[...], axis=0)
    spread_out(2, g1, i1, peer1, lambda p: res.at[i1], res.at[i1])

    total = res[...].reshape(128, 128)
    lanes = lax.broadcasted_iota(jnp.int32, (48, 128), 1)
    first = pltpu.roll(total[0:48], 16, 1)
    last = pltpu.roll(total[48:96], 32, 1)
    rest = jnp.where(lanes < 16, first, last) * scales[1]
    for ky in range(3):
        part = total * scales[1]
        part = pltpu.roll(part, 128 - 32 * ky, 1) if ky else part
        whole = jnp.concatenate([part, rest[ky * 16 : ky * 16 + 16]], axis=0)[:, 0:32]
        for kx in range(3):
            out_g2[kx, ky] = whole[kx * 48 : kx * 48 + 48].reshape(3, 16, 32)
    flat[...] = pltpu.roll(total, 32, 1) * scales[0]
    for kx in range(3):
        for ky in range(3):
            for kz in range(3):
                row = ky * 40 + kz * 12 + kx * 4
                out_g1[kx, ky, kz] = flat[row : row + 4, 0:16]

    for s in range(2):
        second[s][1].wait()
        third[s].wait()


def solution(mesh):
    sizes = (space_grid(mesh.shape["space"]), mesh.shape["batch"])

    def body(volumes, first_kernel, second_kernel, cotangent):
        cells = math.prod(volumes.shape) // volumes.shape[1] * mesh.size
        scales = (1.0 / math.sqrt(cells), 1.0 / math.sqrt(cells / 8))
        w1 = jnp.transpose(first_kernel, (2, 3, 4, 1, 0))
        w2 = jnp.transpose(second_kernel, (2, 3, 4, 1, 0))
        anywhere = pl.BlockSpec(memory_space=pl.ANY)
        vmem = pl.BlockSpec(memory_space=pltpu.VMEM)
        g1 = sizes[0][0] * sizes[0][2]
        g2 = sizes[0][1] * sizes[1]
        act, pooled_grad, grad1, grad2 = pl.pallas_call(
            functools.partial(kernel, sizes, scales),
            out_shape=(
                jax.ShapeDtypeStruct((2, 32, 2, 8, 128), BF16),
                jax.ShapeDtypeStruct((2, 16, 2, 8, 128), BF16),
                jax.ShapeDtypeStruct((3, 3, 3, 4, 16), F32),
                jax.ShapeDtypeStruct((3, 3, 3, 16, 32), F32),
            ),
            in_specs=[anywhere, vmem, vmem, anywhere],
            out_specs=(anywhere, anywhere, vmem, vmem),
            scratch_shapes=[
                pltpu.VMEM((2, 6, 4, 16, 256), BF16),
                pltpu.VMEM((2, 384, 128), F32),
                pltpu.VMEM((2, 1456, 256), BF16),
                pltpu.VMEM((2, 1024, 256), F32),
                pltpu.VMEM((2, 8, 2, 16, 128), BF16),
                pltpu.VMEM((2, 2, 8, 16, 128), BF16),
                pltpu.VMEM((2, 1984, 128), BF16),
                pltpu.VMEM((2, 32, 2, 8, 128), BF16),
                pltpu.VMEM((512, 128), F32),
                pltpu.VMEM((512, 128), F32),
                pltpu.VMEM((2, 32, 2, 8, 128), BF16),
                pltpu.VMEM((2, 8, 2, 32, 128), BF16),
                pltpu.VMEM((2, 2, 8, 32, 128), BF16),
                pltpu.VMEM((2, 3840, 128), BF16),
                pltpu.VMEM((256, 128), F32),
                pltpu.VMEM((2, 16, 2, 8, 128), BF16),
                pltpu.VMEM((256, 128), F32),
                pltpu.VMEM((640, 128), F32),
                pltpu.VMEM((432, 128), F32),
                pltpu.VMEM((64, 256), BF16),
                pltpu.VMEM((64, 640), BF16),
                pltpu.VMEM((32, 1152), BF16),
                pltpu.VMEM((256, 128), F32),
                pltpu.VMEM((576, 128), F32),
                pltpu.VMEM((16, 8, 128), F32),
                pltpu.VMEM((g1, 16 // g1, 8, 128), F32),
                pltpu.VMEM((g2, 16 // g1, 8, 128), F32),
                pltpu.VMEM((g1, 16 // g1, 8, 128), F32),
                pltpu.VMEM((128, 128), F32),
                pltpu.SemaphoreType.DMA((13,)),
                pltpu.SemaphoreType.DMA((6, 2)),
                pltpu.SemaphoreType.DMA((6, 2)),
                pltpu.SemaphoreType.DMA((3, max(g1, g2))),
                pltpu.SemaphoreType.DMA((3, max(g1, g2))),
            ],
            compiler_params=pltpu.CompilerParams(
                collective_id=0, has_side_effects=True, vmem_limit_bytes=40 * 1024 * 1024
            ),
        )(volumes, w1, w2, cotangent)
        return (
            act,
            pooled_grad,
            jnp.transpose(grad1, (4, 3, 0, 1, 2)),
            jnp.transpose(grad2, (4, 3, 0, 1, 2)),
        )

    return jax.shard_map(
        body,
        mesh=mesh,
        in_specs=(
            P("batch", None, "space", None, None),
            P(),
            P(),
            P("batch", None, "space", None, None),
        ),
        out_specs=(
            P("batch", None, "space", None, None),
            P("batch", None, "space", None, None),
            P(),
            P(),
        ),
        check_vma=False,
    )
```

```python
import functools
import math

import jax
import jax.numpy as jnp
from jax import lax
from jax.experimental import pallas as pl
from jax.experimental.pallas import tpu as pltpu
from jax.sharding import PartitionSpec as P

F32 = jnp.float32
BF16 = jnp.bfloat16
MESH = pl.DeviceIdType.MESH


def space_grid(count):
    side = round(count ** (1 / 3))
    if side**3 == count:
        return side, side, side
    return 2, 1, count // 2


def dot(a, b):
    return jnp.dot(a, b, preferred_element_type=F32)


def dot_nt(a, b):
    return lax.dot_general(a, b, (((1,), (1,)), ((), ())), preferred_element_type=F32)


def shifts(v):
    lanes = lax.broadcasted_iota(jnp.int32, v.shape, 1)
    width = v.shape[1]
    before = jnp.where(lanes == 0, 0.0, pltpu.roll(v, 1, 1))
    after = jnp.where(lanes == width - 1, 0.0, pltpu.roll(v, width - 1, 1))
    return before, after


def split(v):
    high = v.astype(BF16)
    return high, (v - high.astype(F32)).astype(BF16)


def act_and_slope(z):
    t = jnp.tanh(0.5 * z)
    a = 0.65 + 0.35 * t
    return z * a, a + (0.175 * z) * (1.0 - t * t)


def kernel(
    sizes, vol, w1_hbm, w2_hbm, cot, out_act, out_pg, out_s1, out_s2,
    vbuf, vf, u1, slope, pb, ph, u2, cotb, ch, cotf, actf, actb, db, u3, bkf, bkb,
    w1, w2, a1s, a2s, w2f, a1, a2, a3, acc1, acc2, pack2, p1, q1, r1, r2, res,
    local_sem, halo_send, halo_recv, sum_send, sum_recv,
):
    (nx, nzh, ny), nb = sizes
    n_space = nx * nzh * ny
    g1, g2 = nx * ny, nzh * nb
    tp = 16 // g1
    sp, bt = lax.axis_index("space"), lax.axis_index("batch")
    xi = lax.div(sp, nzh * ny)
    zi = lax.rem(lax.div(sp, ny), nzh)
    yi = lax.rem(sp, ny)
    i1 = xi * ny + yi
    i2 = zi * nb + bt
    right = lax.rem(sp + 1, n_space)
    left = lax.rem(sp + n_space - 1, n_space)

    def peer1(p):
        return (lax.div(p, ny) * (nzh * ny) + zi * ny + lax.rem(p, ny), bt)

    def peer2(p):
        return (xi * (nzh * ny) + lax.div(p, nb) * ny + yi, lax.rem(p, nb))

    barrier = pltpu.get_barrier_semaphore()
    for side in (left, right):
        pl.semaphore_signal(barrier, inc=1, device_id=(side, bt), device_id_type=MESH)

    def greet1(d, c):
        pl.semaphore_signal(barrier, inc=1, device_id=peer1(lax.rem(i1 + d, g1)), device_id_type=MESH)
        return c

    def greet2(d, c):
        pl.semaphore_signal(barrier, inc=1, device_id=peer2(lax.rem(i2 + d, g2)), device_id_type=MESH)
        return c

    lax.fori_loop(1, g1, greet1, 0)
    lax.fori_loop(1, g2, greet2, 0)

    own = []
    for s in range(2):
        for x in range(4):
            own.append(pltpu.make_async_copy(vol.at[s, :, x], vbuf.at[s, x + 1], local_sem.at[s * 4 + x]))
    own.append(pltpu.make_async_copy(cot, cotb, local_sem.at[8]))
    own.append(pltpu.make_async_copy(w1_hbm, w1, local_sem.at[13]))
    own.append(pltpu.make_async_copy(w2_hbm, w2, local_sem.at[14]))
    for c in own:
        c.start()
    for c in own[0:8]:
        c.wait()

    pl.semaphore_wait(barrier, 2 + g1 - 1 + g2 - 1)

    def both_ways(k, to_right, land_right, to_left, land_left):
        one = pltpu.make_async_remote_copy(
            src_ref=to_right, dst_ref=land_right, send_sem=halo_send.at[k, 0], recv_sem=halo_recv.at[k, 0],
            device_id=(right, bt), device_id_type=MESH,
        )
        two = pltpu.make_async_remote_copy(
            src_ref=to_left, dst_ref=land_left, send_sem=halo_send.at[k, 1], recv_sem=halo_recv.at[k, 1],
            device_id=(left, bt), device_id_type=MESH,
        )
        return one, two

    halos = [both_ways(s, vbuf.at[s, 4], vbuf.at[s, 0], vbuf.at[s, 1], vbuf.at[s, 5]) for s in range(2)]
    for pair in halos:
        for c in pair:
            c.start()
    for c in own[8:]:
        c.wait()
    cot_pairs = [both_ways(4 + s, cotb.at[s, :, 1], ch.at[s, 0], cotb.at[s, :, 0], ch.at[s, 1]) for s in range(2)]
    for pair in cot_pairs:
        for c in pair:
            c.start()

    def arrive(pair, low, high):
        for c in pair:
            c.wait()

        @pl.when(sp == 0)
        def _():
            low[...] = jnp.zeros_like(low)

        @pl.when(sp == n_space - 1)
        def _():
            high[...] = jnp.zeros_like(high)

    a1s[...] = jnp.zeros_like(a1s)
    for kx in range(3):
        for ky in range(3):
            for kz in range(3):
                row = ky * 80 + kz * 24 + kx * 4
                a1s[row : row + 4, 0:16] = w1[kx, ky, kz].astype(F32)
    base = a1s[...]
    t1 = base
    for x in range(1, 4):
        t1 = t1 + pltpu.roll(pltpu.roll(base, 4 * x, 0), 16 * x, 1)
    a1[...] = t1.T[0:64].astype(BF16)

    w2f[...] = jnp.zeros_like(w2f)
    w2f[:, 0:32] = w2[...].reshape(432, 32).astype(F32)
    a2s[...] = jnp.zeros_like(a2s)
    for ky in range(3):
        for kx in range(3):
            a2s[ky * 288 + kx * 48 : ky * 288 + kx * 48 + 48, :] = w2f[(kx * 3 + ky) * 48 : (kx * 3 + ky) * 48 + 48, :]
    base = a2s[...]
    t2 = base
    for x in range(1, 4):
        t2 = t2 + pltpu.roll(pltpu.roll(base, 48 * x, 0), 32 * x, 1)
    a2[...] = t2.T.astype(BF16)
    for ky in range(3):
        for kz in range(3):
            rows = [((kx * 3 + 2 - ky) * 3 + 2 - kz) * 16 for kx in range(3)]
            blocks = [w2f[r : r + 16, :] for r in rows]
            first = blocks[2] + pltpu.roll(blocks[1], 32, 1) + pltpu.roll(blocks[0], 64, 1)
            both = jnp.concatenate([first, pltpu.roll(first, 32, 1)], axis=0)
            a3[:, (ky * 3 + kz) * 128 : (ky * 3 + kz) * 128 + 128] = both.astype(BF16)

    zrow = lax.broadcasted_iota(jnp.int32, (256, 128), 0)
    zcol = lax.broadcasted_iota(jnp.int32, (256, 128), 1)
    halve = jnp.where(lax.div(zrow, 2) == zcol, 0.125, 0.0).astype(BF16)
    zrow = lax.broadcasted_iota(jnp.int32, (128, 256), 0)
    zcol = lax.broadcasted_iota(jnp.int32, (128, 256), 1)
    double = jnp.where(zrow == lax.div(zcol, 2), 1.0, 0.0).astype(BF16)

    acc1[...] = jnp.zeros_like(acc1)
    acc2[...] = jnp.zeros_like(acc2)
    for s in range(2):
        u1[s, 0:80, :] = jnp.zeros((80, 256), BF16)
        u1[s, 1360:1456, :] = jnp.zeros((96, 256), BF16)
        u2[s, 0:288, :] = jnp.zeros((288, 128), BF16)
        u2[s, 2592:2912, :] = jnp.zeros((320, 128), BF16)
        u3[s, 0:384, :] = jnp.zeros((384, 128), BF16)
        u3[s, 3456:3840, :] = jnp.zeros((384, 128), BF16)

    def stage1(s):
        arrive(halos[s], vbuf.at[s, 0], vbuf.at[s, 5])
        planes = vbuf[s].reshape(384, 256).astype(F32)
        for half in range(2):
            vf[half] = planes[:, 128 * half : 128 * half + 128]

        def fill(y, c):
            v = jnp.concatenate([vf[half, pl.ds(y, 24, stride=16), :] for half in range(2)], axis=1)
            before, after = shifts(v)
            rows = jnp.concatenate([before, v, after, jnp.zeros((8, 256), F32)], axis=0)
            u1[s, pl.ds(pl.multiple_of((y + 1) * 80, 16), 80), :] = rows.astype(BF16)
            return c

        lax.fori_loop(0, 16, fill, 0, unroll=4)

        def forward(j, c):
            total = None
            for i in range(2):
                y = 2 * j + i
                pre = dot(a1[...], u1[s, pl.ds(pl.multiple_of(y * 80, 16), 256), :])
                act, sl = act_and_slope(pre)
                slope[s, pl.ds(pl.multiple_of(y * 64, 64), 64), :] = 0.125 * sl
                total = act if total is None else total + act
            pairs = jnp.concatenate([total[0:16] + total[16:32], total[32:48] + total[48:64]], axis=0)
            high, low = split(pairs)
            pooled = (dot(high, halve) + dot(low, halve)).astype(BF16)
            pb[s, j] = pooled.reshape(2, 16, 128)
            mid = pooled.astype(F32)
            before, after = shifts(mid)
            for x in range(2):
                part = slice(16 * x, 16 * x + 16)
                rows = jnp.concatenate([before[part], mid[part], after[part]], axis=0)
                u2[s, pl.ds(pl.multiple_of((j + 1) * 288 + (x + 2) * 48, 16), 48), :] = rows.astype(BF16)
            return c

        lax.fori_loop(0, 8, forward, 0, unroll=4)
        pair = both_ways(2 + s, pb.at[s], ph.at[s, 0], pb.at[s], ph.at[s, 1])
        for c in pair:
            c.start()
        return pair

    def stage2(s, pair):
        for x in range(2):
            cotf[x + 1] = cotb[s, :, x].reshape(256, 128).astype(F32)
        arrive(cot_pairs[s], ch.at[s, 0], ch.at[s, 1])
        for side in range(2):
            cotf[3 * side] = ch[s, side].reshape(256, 128).astype(F32)
        arrive(pair, ph.at[s, 0], ph.at[s, 1])

        def fill(j, c):
            for side in range(2):
                mid = ph[s, side, j].reshape(32, 128).astype(F32)
                before, after = shifts(mid)
                for x in range(2):
                    part = slice(16 * x, 16 * x + 16)
                    rows = jnp.concatenate([before[part], mid[part], after[part]], axis=0)
                    at = pl.multiple_of((j + 1) * 288 + (side * 4 + x) * 48, 16)
                    u2[s, pl.ds(at, 48), :] = rows.astype(BF16)
            return c

        lax.fori_loop(0, 8, fill, 0, unroll=4)

        def forward(j, c):
            pre = dot(a2[...], u2[s, pl.ds(pl.multiple_of(j * 288, 32), 896), :])
            act, sl = act_and_slope(pre)
            for x in range(2):
                actf[pl.ds(x * 8 + j, 32, stride=16), :] = act[32 + 32 * x : 64 + 32 * x]
            got = [cotf[x, pl.ds(j, 32, stride=8), :] for x in range(4)]
            delta = (jnp.concatenate(got, axis=0) * sl).astype(BF16)
            db[s, j] = delta[32:96]
            mid = delta.astype(F32)
            before, after = shifts(mid)
            for kz, rows in enumerate((before, mid, after)):
                u3[s, pl.ds(pl.multiple_of((j + 1) * 384 + kz * 128, 128), 128), :] = rows.astype(BF16)
            return c

        lax.fori_loop(0, 8, forward, 0, unroll=4)
        actb[s] = actf[...].reshape(32, 2, 8, 128).astype(BF16)
        act_copy = pltpu.make_async_copy(actb.at[s], out_act.at[s], local_sem.at[9 + s])
        act_copy.start()
        return act_copy

    def second_grad(s):
        def grad(j, c):
            fields, deltas = [], []
            for i in range(2):
                y = 2 * j + i
                rows = [u2[s, pl.ds(pl.multiple_of((y + ky) * 288 + 48, 16), 192), :] for ky in range(3)]
                fields.append(jnp.concatenate(rows, axis=0))
                deltas.append(db[s, y])
            acc2[:, 0:64] += dot_nt(jnp.concatenate(fields, axis=1), jnp.concatenate(deltas, axis=1))
            return c

        lax.fori_loop(0, 4, grad, 0, unroll=2)

    def stage3(s):
        def backward(j, c):
            back = dot(a3[...], u3[s, pl.ds(pl.multiple_of(j * 384, 128), 1152), :])
            for x in range(2):
                bkf[pl.ds(x * 8 + j, 16, stride=16), :] = back[16 * x : 16 * x + 16]
            high, low = split(back)
            up = dot(high, double) + dot(low, double)
            up = jnp.concatenate([up[0:16], up[0:16], up[16:32], up[16:32]], axis=0)
            fields, deltas = [], []
            for i in range(2):
                y = 2 * j + i
                deltas.append((up * slope[s, pl.ds(pl.multiple_of(y * 64, 64), 64), :]).astype(BF16))
                fields.append(u1[s, pl.ds(pl.multiple_of(y * 80, 16), 256), :])
            acc1[:, 0:64] += dot_nt(jnp.concatenate(fields, axis=1), jnp.concatenate(deltas, axis=1))
            return c

        lax.fori_loop(0, 8, backward, 0, unroll=4)
        bkb[s] = bkf[...].reshape(16, 2, 8, 128).astype(BF16)
        copy = pltpu.make_async_copy(bkb.at[s], out_pg.at[s], local_sem.at[11 + s])
        copy.start()
        return copy

    def exchange(phase, group, index, peer, src, dst):
        def make(d):
            other = lax.rem(index + d, group)
            return pltpu.make_async_remote_copy(
                src_ref=src(other), dst_ref=dst, send_sem=sum_send.at[phase, d], recv_sem=sum_recv.at[phase, d],
                device_id=peer(other), device_id_type=MESH,
            )

        def go(d, c):
            make(d).start()
            return c

        def end(d, c):
            make(d).wait()
            return c

        lax.fori_loop(1, group, go, 0)
        return lambda: lax.fori_loop(1, group, end, 0)

    pooled_pairs = [stage1(0), stage1(1)]
    copies = []
    for s in range(2):
        copies.append(stage2(s, pooled_pairs[s]))
        if s == 0:
            copies.append(stage3(0))
        second_grad(s)

    lanes = lax.broadcasted_iota(jnp.int32, (432, 128), 1)
    g = acc2[...].reshape(3, 192, 128)
    upper = g[:, 48:192].reshape(432, 128)
    f2 = jnp.where(lanes < 32, g[:, 0:144].reshape(432, 128) + pltpu.roll(upper, 96, 1), 0.0)
    packed = f2[0:128]
    rest = [f2[128:144]]
    for ky in range(1, 3):
        packed = packed + pltpu.roll(f2[ky * 144 : ky * 144 + 128], 32 * ky, 1)
        rest.append(f2[ky * 144 + 128 : ky * 144 + 144])
    rest = pltpu.roll(jnp.concatenate(rest, axis=0), 96, 1)
    packed = packed + jnp.concatenate([rest, jnp.zeros((80, 128), F32)], axis=0)
    pack2[...] = packed.reshape(16, 8, 128)

    r1[i1] = pack2[pl.ds(i1 * tp, tp)]
    scattered = exchange(0, g1, i1, peer1, lambda p: pack2.at[pl.ds(p * tp, tp)], r1.at[i1])

    copies.append(stage3(1))

    g = acc1[0:240, :]
    f1 = g
    for x in range(1, 4):
        f1 = f1 + pltpu.roll(pltpu.roll(g, 240 - 4 * x, 0), 128 - 16 * x, 1)
    rows = lax.rem(lax.broadcasted_iota(jnp.int32, (240, 128), 0), 80)
    f1 = jnp.where(lax.broadcasted_iota(jnp.int32, (240, 128), 1) < 16, f1, 0.0)
    f1c = None
    for kz in range(3):
        part = jnp.where((rows >= 24 * kz) & (rows < 24 * kz + 12), f1, 0.0)
        part = pltpu.roll(part, 240 - 12 * kz, 0) if kz else part
        f1c = part if f1c is None else f1c + part
    f1c = f1c.reshape(3, 80, 128)[:, 0:40].reshape(120, 128)
    f1c = jnp.concatenate([f1c, jnp.zeros((8, 128), F32)], axis=0)
    packed = f1c[0:16]
    for k in range(1, 8):
        packed = packed + pltpu.roll(f1c[16 * k : 16 * k + 16], 16 * k, 1)
    p1[i1] = packed
    within = exchange(3, g1, i1, peer1, lambda p: p1.at[i1], p1.at[i1])
    scattered()
    r2[i2] = jnp.sum(r1[...], axis=0)
    crossed = exchange(1, g2, i2, peer2, lambda p: r2.at[i2], r2.at[i2])
    within()
    q1[i2] = jnp.sum(p1[...], axis=0)
    over = exchange(4, g2, i2, peer2, lambda p: q1.at[i2], q1.at[i2])
    crossed()
    res[i1] = jnp.sum(r2[...], axis=0)
    gathered = exchange(2, g1, i1, peer1, lambda p: res.at[i1], res.at[i1])
    over()
    out_s1[...] = jnp.sum(q1[...], axis=0)
    gathered()
    out_s2[...] = res[...].reshape(128, 128)
    for c in copies:
        c.wait()


def finish(
    scales, act, pg, s1, s2, out_act, out_pg, out_g1, out_g2, actv, pgv, sums1, sums2, flat, g1v, g2v, sem
):
    loads = [
        pltpu.make_async_copy(src, dst, sem.at[k])
        for k, (src, dst) in enumerate(((s1, sums1), (s2, sums2), (act, actv), (pg, pgv)))
    ]
    stores = [
        pltpu.make_async_copy(src, dst, sem.at[4 + k])
        for k, (src, dst) in enumerate(((actv, out_act), (pgv, out_pg), (g1v, out_g1), (g2v, out_g2)))
    ]
    for c in loads:
        c.start()
    for k in (2, 3):
        loads[k].wait()
        stores[k - 2].start()
    for c in loads[0:2]:
        c.wait()
    total = sums2[...] * scales[1]
    rest = pltpu.roll(total[0:48], 32, 1)
    for ky in range(3):
        part = pltpu.roll(total, 128 - 32 * ky, 1) if ky else total
        whole = jnp.concatenate([part, rest[ky * 16 : ky * 16 + 16]], axis=0)[:, 0:32]
        for kx in range(3):
            g2v[kx, ky] = whole[kx * 48 : kx * 48 + 48].reshape(3, 16, 32)
    total = sums1[...] * scales[0]
    for k in range(8):
        flat[16 * k : 16 * k + 16, :] = pltpu.roll(total, 128 - 16 * k, 1) if k else total
    for kx in range(3):
        for ky in range(3):
            for kz in range(3):
                row = ky * 40 + kz * 12 + kx * 4
                g1v[kx, ky, kz] = flat[row : row + 4, 0:16]
    for c in stores[2:]:
        c.start()
    for c in stores:
        c.wait()


def solution(mesh):
    sizes = (space_grid(mesh.shape["space"]), mesh.shape["batch"])

    def body(volumes, first_kernel, second_kernel, cotangent):
        cells = math.prod(volumes.shape) // volumes.shape[1] * mesh.size
        scales = (1.0 / math.sqrt(cells), 1.0 / math.sqrt(cells / 8))
        w1 = jnp.transpose(first_kernel, (2, 3, 4, 1, 0))
        w2 = jnp.transpose(second_kernel, (2, 3, 4, 1, 0))
        hbm = pl.BlockSpec(memory_space=pltpu.HBM)
        g1 = sizes[0][0] * sizes[0][2]
        g2 = sizes[0][1] * sizes[1]
        vmem_limit = 60 * 1024 * 1024
        act, pooled_grad, sums1, sums2 = pl.pallas_call(
            functools.partial(kernel, sizes),
            out_shape=(
                jax.ShapeDtypeStruct((2, 32, 2, 8, 128), BF16),
                jax.ShapeDtypeStruct((2, 16, 2, 8, 128), BF16),
                jax.ShapeDtypeStruct((16, 128), F32),
                jax.ShapeDtypeStruct((128, 128), F32),
            ),
            in_specs=[hbm] * 4,
            out_specs=(hbm, hbm, pl.BlockSpec(memory_space=pltpu.VMEM), pl.BlockSpec(memory_space=pltpu.VMEM)),
            scratch_shapes=[
                pltpu.VMEM((2, 6, 4, 16, 256), BF16),
                pltpu.VMEM((2, 384, 128), F32),
                pltpu.VMEM((2, 1456, 256), BF16),
                pltpu.VMEM((2, 1024, 256), F32),
                pltpu.VMEM((2, 8, 2, 16, 128), BF16),
                pltpu.VMEM((2, 2, 8, 2, 16, 128), BF16),
                pltpu.VMEM((2, 2912, 128), BF16),
                pltpu.VMEM((2, 32, 2, 8, 128), BF16),
                pltpu.VMEM((2, 2, 32, 8, 128), BF16),
                pltpu.VMEM((4, 256, 128), F32),
                pltpu.VMEM((512, 128), F32),
                pltpu.VMEM((2, 32, 2, 8, 128), BF16),
                pltpu.VMEM((2, 8, 64, 128), BF16),
                pltpu.VMEM((2, 3840, 128), BF16),
                pltpu.VMEM((256, 128), F32),
                pltpu.VMEM((2, 16, 2, 8, 128), BF16),
                pltpu.VMEM((3, 3, 3, 4, 16), BF16),
                pltpu.VMEM((3, 3, 3, 16, 32), BF16),
                pltpu.VMEM((256, 128), F32),
                pltpu.VMEM((896, 128), F32),
                pltpu.VMEM((432, 128), F32),
                pltpu.VMEM((64, 256), BF16),
                pltpu.VMEM((128, 896), BF16),
                pltpu.VMEM((32, 1152), BF16),
                pltpu.VMEM((256, 128), F32),
                pltpu.VMEM((576, 128), F32),
                pltpu.VMEM((16, 8, 128), F32),
                pltpu.VMEM((g1, 16, 128), F32),
                pltpu.VMEM((g2, 16, 128), F32),
                pltpu.VMEM((g1, 16 // g1, 8, 128), F32),
                pltpu.VMEM((g2, 16 // g1, 8, 128), F32),
                pltpu.VMEM((g1, 16 // g1, 8, 128), F32),
                pltpu.SemaphoreType.DMA((15,)),
                pltpu.SemaphoreType.DMA((6, 2)),
                pltpu.SemaphoreType.DMA((6, 2)),
                pltpu.SemaphoreType.DMA((5, max(g1, g2))),
                pltpu.SemaphoreType.DMA((5, max(g1, g2))),
            ],
            compiler_params=pltpu.CompilerParams(
                collective_id=0, has_side_effects=True, vmem_limit_bytes=vmem_limit
            ),
        )(volumes, w1, w2, cotangent)
        act, pooled_grad, grad1, grad2 = pl.pallas_call(
            functools.partial(finish, scales),
            out_shape=(
                jax.ShapeDtypeStruct((2, 32, 2, 8, 128), BF16),
                jax.ShapeDtypeStruct((2, 16, 2, 8, 128), BF16),
                jax.ShapeDtypeStruct((3, 3, 3, 4, 16), F32),
                jax.ShapeDtypeStruct((3, 3, 3, 16, 32), F32),
            ),
            in_specs=[hbm] * 4,
            out_specs=(hbm,) * 4,
            scratch_shapes=[
                pltpu.VMEM((2, 32, 2, 8, 128), BF16),
                pltpu.VMEM((2, 16, 2, 8, 128), BF16),
                pltpu.VMEM((16, 128), F32),
                pltpu.VMEM((128, 128), F32),
                pltpu.VMEM((128, 128), F32),
                pltpu.VMEM((3, 3, 3, 4, 16), F32),
                pltpu.VMEM((3, 3, 3, 16, 32), F32),
                pltpu.SemaphoreType.DMA((8,)),
            ],
            compiler_params=pltpu.CompilerParams(vmem_limit_bytes=vmem_limit),
        )(act, pooled_grad, sums1, sums2)
        return (
            act,
            pooled_grad,
            jnp.transpose(grad1, (4, 3, 0, 1, 2)),
            jnp.transpose(grad2, (4, 3, 0, 1, 2)),
        )

    return jax.shard_map(
        body,
        mesh=mesh,
        in_specs=(
            P("batch", None, "space", None, None),
            P(),
            P(),
            P("batch", None, "space", None, None),
        ),
        out_specs=(
            P("batch", None, "space", None, None),
            P("batch", None, "space", None, None),
            P(),
            P(),
        ),
        check_vma=False,
    )
```

```python
import functools
import math

import jax
import jax.numpy as jnp
from jax import lax
from jax.experimental import pallas as pl
from jax.experimental.pallas import tpu as pltpu
from jax.sharding import PartitionSpec as P

F32 = jnp.float32
BF16 = jnp.bfloat16
MESH = pl.DeviceIdType.MESH


def space_grid(count):
    side = round(count ** (1 / 3))
    if side**3 == count:
        return side, side, side
    return 2, 1, count // 2


def dot(a, b):
    return jnp.dot(a, b, preferred_element_type=F32)


def dot_nt(a, b):
    return lax.dot_general(a, b, (((1,), (1,)), ((), ())), preferred_element_type=F32)


def shifts(v):
    lanes = lax.broadcasted_iota(jnp.int32, v.shape, 1)
    width = v.shape[1]
    before = jnp.where(lanes == 0, 0.0, pltpu.roll(v, 1, 1))
    after = jnp.where(lanes == width - 1, 0.0, pltpu.roll(v, width - 1, 1))
    return before, after


def pair_sums(v):
    first, second = v[:, 0:128], v[:, 128:256]
    lanes = lax.broadcasted_iota(jnp.int32, first.shape, 1)
    mixed = jnp.where(
        (lanes & 1) == 0, first + pltpu.roll(first, 127, 1), second + pltpu.roll(second, 1, 1)
    )
    source = jnp.where(lanes < 64, 2 * lanes, 2 * lanes - 127)
    return jnp.take_along_axis(mixed, source, axis=1)


def doubled(v):
    lanes = lax.broadcasted_iota(jnp.int32, v.shape, 1)
    half = lanes >> 1
    return [jnp.take_along_axis(v, half, axis=1), jnp.take_along_axis(v, half + 64, axis=1)]


def act_and_slope(z):
    t = jnp.tanh(0.5 * z)
    a = 0.65 + 0.35 * t
    return z * a, a + (0.175 * z) * (1.0 - t * t)


def kernel(
    sizes, vol, w1_hbm, w2_hbm, cot, out_act, out_pg, out_s1, out_s2,
    vbuf, vf, u1, slope, pb, ph, u2, cotb, ch, cotf, actf, actb, db, fd, u3, bkf, bkb,
    w1, w2, a1s, a2s, w2f, a1, a2, a3, acc1, acc2, pack2, p1, q1, r1, r2, res,
    local_sem, halo_send, halo_recv, sum_send, sum_recv,
):
    (nx, nzh, ny), nb = sizes
    n_space = nx * nzh * ny
    g1, g2 = nx * ny, nzh * nb
    tp = 16 // g1
    sp, bt = lax.axis_index("space"), lax.axis_index("batch")
    xi = lax.div(sp, nzh * ny)
    zi = lax.rem(lax.div(sp, ny), nzh)
    yi = lax.rem(sp, ny)
    i1 = xi * ny + yi
    i2 = zi * nb + bt
    right = lax.rem(sp + 1, n_space)
    left = lax.rem(sp + n_space - 1, n_space)

    def peer1(p):
        return (lax.div(p, ny) * (nzh * ny) + zi * ny + lax.rem(p, ny), bt)

    def peer2(p):
        return (xi * (nzh * ny) + lax.div(p, nb) * ny + yi, lax.rem(p, nb))

    barrier = pltpu.get_barrier_semaphore()
    for side in (left, right):
        pl.semaphore_signal(barrier, inc=1, device_id=(side, bt), device_id_type=MESH)

    def greet1(d, c):
        pl.semaphore_signal(barrier, inc=1, device_id=peer1(lax.rem(i1 + d, g1)), device_id_type=MESH)
        return c

    def greet2(d, c):
        pl.semaphore_signal(barrier, inc=1, device_id=peer2(lax.rem(i2 + d, g2)), device_id_type=MESH)
        return c

    lax.fori_loop(1, g1, greet1, 0)
    lax.fori_loop(1, g2, greet2, 0)

    own = []
    for s in range(2):
        for x in range(4):
            own.append(pltpu.make_async_copy(vol.at[s, :, x], vbuf.at[s, x + 1], local_sem.at[s * 4 + x]))
    own.append(pltpu.make_async_copy(cot, cotb, local_sem.at[8]))
    own.append(pltpu.make_async_copy(w1_hbm, w1, local_sem.at[13]))
    own.append(pltpu.make_async_copy(w2_hbm, w2, local_sem.at[14]))
    for c in own:
        c.start()
    for c in own[0:8]:
        c.wait()

    pl.semaphore_wait(barrier, 2 + g1 - 1 + g2 - 1)

    def both_ways(k, to_right, land_right, to_left, land_left):
        one = pltpu.make_async_remote_copy(
            src_ref=to_right, dst_ref=land_right, send_sem=halo_send.at[k, 0], recv_sem=halo_recv.at[k, 0],
            device_id=(right, bt), device_id_type=MESH,
        )
        two = pltpu.make_async_remote_copy(
            src_ref=to_left, dst_ref=land_left, send_sem=halo_send.at[k, 1], recv_sem=halo_recv.at[k, 1],
            device_id=(left, bt), device_id_type=MESH,
        )
        return one, two

    halos = [both_ways(s, vbuf.at[s, 4], vbuf.at[s, 0], vbuf.at[s, 1], vbuf.at[s, 5]) for s in range(2)]
    for pair in halos:
        for c in pair:
            c.start()
    for c in own[8:]:
        c.wait()
    cot_pairs = [both_ways(4 + s, cotb.at[s, :, 1], ch.at[s, 0], cotb.at[s, :, 0], ch.at[s, 1]) for s in range(2)]
    for pair in cot_pairs:
        for c in pair:
            c.start()

    def arrive(pair, low, high):
        for c in pair:
            c.wait()

        @pl.when(sp == 0)
        def _():
            low[...] = jnp.zeros_like(low)

        @pl.when(sp == n_space - 1)
        def _():
            high[...] = jnp.zeros_like(high)

    a1s[...] = jnp.zeros_like(a1s)
    for kx in range(3):
        for ky in range(3):
            for kz in range(3):
                row = ky * 80 + kz * 24 + kx * 4
                a1s[row : row + 4, 0:16] = w1[kx, ky, kz].astype(F32)
    base = a1s[...]
    t1 = base
    for x in range(1, 4):
        t1 = t1 + pltpu.roll(pltpu.roll(base, 4 * x, 0), 16 * x, 1)
    a1[...] = t1.T[0:64].astype(BF16)

    w2f[...] = jnp.zeros_like(w2f)
    w2f[:, 0:32] = w2[...].reshape(432, 32).astype(F32)
    a2s[...] = jnp.zeros_like(a2s)
    for ky in range(3):
        for kx in range(3):
            a2s[ky * 288 + kx * 48 : ky * 288 + kx * 48 + 48, :] = w2f[(kx * 3 + ky) * 48 : (kx * 3 + ky) * 48 + 48, :]
    base = a2s[...]
    t2 = base
    for x in range(1, 4):
        t2 = t2 + pltpu.roll(pltpu.roll(base, 48 * x, 0), 32 * x, 1)
    a2[...] = t2.T.astype(BF16)
    for ky in range(3):
        for kz in range(3):
            rows = [((kx * 3 + 2 - ky) * 3 + 2 - kz) * 16 for kx in range(3)]
            blocks = [w2f[r : r + 16, :] for r in rows]
            first = blocks[2] + pltpu.roll(blocks[1], 32, 1) + pltpu.roll(blocks[0], 64, 1)
            both = jnp.concatenate([first, pltpu.roll(first, 32, 1)], axis=0)
            a3[32 * ky : 32 * ky + 32, kz * 128 : kz * 128 + 128] = both.astype(BF16)

    for s in range(2):
        u1[s, 0:80, :] = jnp.zeros((80, 256), BF16)
        u1[s, 1360:1456, :] = jnp.zeros((96, 256), BF16)
        u2[s, 0:288, :] = jnp.zeros((288, 128), BF16)
        u2[s, 2592:2912, :] = jnp.zeros((320, 128), BF16)
        for y in (0, 9):
            db[s, y] = jnp.zeros((64, 128), BF16)
        for y in (0, 17):
            fd[s, y] = jnp.zeros((64, 256), BF16)

    def stage1(s):
        arrive(halos[s], vbuf.at[s, 0], vbuf.at[s, 5])
        planes = vbuf[s].reshape(384, 256).astype(F32)
        for half in range(2):
            vf[half] = planes[:, 128 * half : 128 * half + 128]
        for y in range(16):
            v = jnp.concatenate([vf[half, pl.ds(y, 24, stride=16), :] for half in range(2)], axis=1)
            before, after = shifts(v)
            rows = jnp.concatenate([before, v, after, jnp.zeros((8, 256), F32)], axis=0)
            u1[s, (y + 1) * 80 : (y + 2) * 80, :] = rows.astype(BF16)
        for j in range(8):
            total = None
            for i in range(2):
                y = 2 * j + i
                pre = dot(a1[...], u1[s, y * 80 : y * 80 + 256, :])
                act, sl = act_and_slope(pre)
                slope[s, y * 64 : y * 64 + 64, :] = 0.125 * sl
                total = act if total is None else total + act
            pairs = jnp.concatenate([total[0:16] + total[16:32], total[32:48] + total[48:64]], axis=0)
            pooled = (0.125 * pair_sums(pairs)).astype(BF16)
            pb[s, j] = pooled.reshape(2, 16, 128)
            mid = pooled.astype(F32)
            before, after = shifts(mid)
            for x in range(2):
                part = slice(16 * x, 16 * x + 16)
                rows = jnp.concatenate([before[part], mid[part], after[part]], axis=0)
                at = (j + 1) * 288 + (x + 2) * 48
                u2[s, at : at + 48, :] = rows.astype(BF16)
        pair = both_ways(2 + s, pb.at[s], ph.at[s, 0], pb.at[s], ph.at[s, 1])
        for c in pair:
            c.start()
        return pair

    def stage2(s, pair):
        for x in range(2):
            cotf[x + 1] = cotb[s, :, x].reshape(256, 128).astype(F32)
        arrive(cot_pairs[s], ch.at[s, 0], ch.at[s, 1])
        for side in range(2):
            cotf[3 * side] = ch[s, side].reshape(256, 128).astype(F32)
        arrive(pair, ph.at[s, 0], ph.at[s, 1])
        for j in range(8):
            for side in range(2):
                mid = ph[s, side, j].reshape(32, 128).astype(F32)
                before, after = shifts(mid)
                for x in range(2):
                    part = slice(16 * x, 16 * x + 16)
                    rows = jnp.concatenate([before[part], mid[part], after[part]], axis=0)
                    at = (j + 1) * 288 + (side * 4 + x) * 48
                    u2[s, at : at + 48, :] = rows.astype(BF16)
        for j in range(8):
            pre = dot(a2[...], u2[s, j * 288 : j * 288 + 896, :])
            act, sl = act_and_slope(pre)
            for x in range(2):
                actf[pl.ds(x * 8 + j, 32, stride=16), :] = act[32 + 32 * x : 64 + 32 * x]
            got = [cotf[x, pl.ds(j, 32, stride=8), :] for x in range(4)]
            delta = (jnp.concatenate(got, axis=0) * sl).astype(BF16)
            db[s, j + 1] = delta[32:96]
            mid = delta.astype(F32)
            before, after = shifts(mid)
            for kz, rows in enumerate((before, mid, after)):
                u3[s, j * 384 + kz * 128 : j * 384 + kz * 128 + 128, :] = rows.astype(BF16)
        actb[s] = actf[...].reshape(32, 2, 8, 128).astype(BF16)
        act_copy = pltpu.make_async_copy(actb.at[s], out_act.at[s], local_sem.at[9 + s])
        act_copy.start()
        return act_copy

    def second_grad(s):
        fields = [u2[s, (y + 1) * 288 + 48 : (y + 1) * 288 + 240, :] for y in range(8)]
        deltas = [db[s, y : y + 3].reshape(192, 128) for y in range(8)]
        return dot_nt(jnp.concatenate(fields, axis=1), jnp.concatenate(deltas, axis=1))

    def stage3(s):
        parts = []
        for j in range(4):
            both = jnp.concatenate([u3[s, (2 * j + i) * 384 : (2 * j + i) * 384 + 384, :] for i in range(2)], axis=1)
            part = dot(a3[...], both)
            parts += [part[:, 0:128], part[:, 128:256]]
        for j in range(8):
            back = parts[j][32:64]
            if j > 0:
                back = back + parts[j - 1][0:32]
            if j < 7:
                back = back + parts[j + 1][64:96]
            for x in range(2):
                bkf[pl.ds(x * 8 + j, 16, stride=16), :] = back[16 * x : 16 * x + 16]
            up = jnp.concatenate(doubled(back), axis=1)
            up = jnp.concatenate([up[0:16], up[0:16], up[16:32], up[16:32]], axis=0)
            for y in (2 * j, 2 * j + 1):
                fd[s, y + 1] = (up * slope[s, y * 64 : y * 64 + 64, :]).astype(BF16)
        bkb[s] = bkf[...].reshape(16, 2, 8, 128).astype(BF16)
        copy = pltpu.make_async_copy(bkb.at[s], out_pg.at[s], local_sem.at[11 + s])
        copy.start()
        return copy

    def first_grad(s):
        total = None
        for k in range(4):
            ys = range(4 * k, 4 * k + 4)
            fields = [u1[s, (y + 1) * 80 : (y + 2) * 80, :] for y in ys]
            deltas = [fd[s, y : y + 3].reshape(192, 256) for y in ys]
            part = dot_nt(jnp.concatenate(fields, axis=1), jnp.concatenate(deltas, axis=1))
            total = part if total is None else total + part
        return total

    def exchange(phase, group, index, peer, src, dst):
        def make(d):
            other = lax.rem(index + d, group)
            return pltpu.make_async_remote_copy(
                src_ref=src(other), dst_ref=dst, send_sem=sum_send.at[phase, d], recv_sem=sum_recv.at[phase, d],
                device_id=peer(other), device_id_type=MESH,
            )

        def go(d, c):
            make(d).start()
            return c

        def end(d, c):
            make(d).wait()
            return c

        lax.fori_loop(1, group, go, 0)
        return lambda: lax.fori_loop(1, group, end, 0)

    pooled_pairs = [stage1(0), stage1(1)]
    copies = [stage2(0, pooled_pairs[0]), stage3(0)]
    acc1[:, 0:192] = first_grad(0)
    acc2[:, 0:192] = second_grad(0)
    copies.append(stage2(1, pooled_pairs[1]))
    acc2[:, 0:192] += second_grad(1)

    lanes = lax.broadcasted_iota(jnp.int32, (144, 128), 1)
    f2 = None
    for f in range(3):
        ky = 2 - f
        tile = acc2[:, 128 * (f // 2) : 128 * (f // 2) + 128]
        move = 32 * ky - 64 * (f % 2)
        part = pltpu.roll(tile[0:144], move % 128, 1) if move % 128 else tile[0:144]
        part = part + pltpu.roll(tile[48:192], (move - 32) % 128, 1)
        part = jnp.where((lanes >= 32 * ky) & (lanes < 32 * ky + 32), part, 0.0)
        f2 = part if f2 is None else f2 + part
    rest = []
    for ky in range(3):
        part = pltpu.roll(f2[128:144], 96 - 32 * ky, 1)
        rest.append(jnp.where(lanes[0:16] >= 96, part, 0.0))
    rest = jnp.concatenate(rest + [jnp.zeros((80, 128), F32)], axis=0)
    pack2[...] = (f2[0:128] + rest).reshape(16, 8, 128)

    r1[i1] = pack2[pl.ds(i1 * tp, tp)]
    scattered = exchange(0, g1, i1, peer1, lambda p: pack2.at[pl.ds(p * tp, tp)], r1.at[i1])

    copies.append(stage3(1))
    acc1[:, 0:192] += first_grad(1)

    rows = lax.broadcasted_iota(jnp.int32, (80, 128), 0)
    lanes = lax.broadcasted_iota(jnp.int32, (80, 128), 1)
    folded = []
    for half in range(2):
        g = acc1[:, 128 * half : 128 * half + 128]
        f1 = g
        for x in range(1, 4):
            f1 = f1 + pltpu.roll(pltpu.roll(g, 80 - 4 * x, 0), 128 - 16 * x, 1)
        f1 = jnp.where((lanes & 63) < 16, f1, 0.0)
        f1c = None
        for kz in range(3):
            part = jnp.where((rows >= 24 * kz) & (rows < 24 * kz + 12), f1, 0.0)
            part = pltpu.roll(part, 80 - 12 * kz, 0) if kz else part
            f1c = part if f1c is None else f1c + part
        folded.append(f1c[0:40])
    packed = [None, None]
    for f in range(3):
        for r in range(5):
            k = f * 5 + r
            part = folded[f // 2][8 * r : 8 * r + 8]
            part = jnp.where((lanes[0:8] >> 6) == f % 2, part, 0.0)
            move = (16 * (k // 2) - 64 * (f % 2)) % 128
            part = pltpu.roll(part, move, 1) if move else part
            packed[k % 2] = part if packed[k % 2] is None else packed[k % 2] + part
    packed = jnp.concatenate(packed, axis=0)
    p1[i1] = packed
    within = exchange(3, g1, i1, peer1, lambda p: p1.at[i1], p1.at[i1])
    scattered()
    r2[i2] = jnp.sum(r1[...], axis=0)
    crossed = exchange(1, g2, i2, peer2, lambda p: r2.at[i2], r2.at[i2])
    within()
    q1[i2] = jnp.sum(p1[...], axis=0)
    over = exchange(4, g2, i2, peer2, lambda p: q1.at[i2], q1.at[i2])
    crossed()
    res[i1] = jnp.sum(r2[...], axis=0)
    gathered = exchange(2, g1, i1, peer1, lambda p: res.at[i1], res.at[i1])
    over()
    out_s1[...] = jnp.sum(q1[...], axis=0)
    gathered()
    out_s2[...] = res[...].reshape(128, 128)
    for c in copies:
        c.wait()


def finish(
    scales, act, pg, s1, s2, out_act, out_pg, out_g1, out_g2, actv, pgv, sums1, sums2, flat, g1v, g2v, sem
):
    loads = [
        pltpu.make_async_copy(src, dst, sem.at[k])
        for k, (src, dst) in enumerate(((s1, sums1), (s2, sums2), (act, actv), (pg, pgv)))
    ]
    stores = [
        pltpu.make_async_copy(src, dst, sem.at[4 + k])
        for k, (src, dst) in enumerate(((actv, out_act), (pgv, out_pg), (g1v, out_g1), (g2v, out_g2)))
    ]
    for c in loads:
        c.start()
    for k in (2, 3):
        loads[k].wait()
        stores[k - 2].start()
    for c in loads[0:2]:
        c.wait()
    total = sums2[...] * scales[1]
    rest = pltpu.roll(total[0:48], 32, 1)
    for ky in range(3):
        part = pltpu.roll(total, 128 - 32 * ky, 1) if ky else total
        whole = jnp.concatenate([part, rest[ky * 16 : ky * 16 + 16]], axis=0)[:, 0:32]
        for kx in range(3):
            g2v[kx, ky] = whole[kx * 48 : kx * 48 + 48].reshape(3, 16, 32)
    total = sums1[...] * scales[0]
    for k in range(15):
        part = total[8 * (k % 2) : 8 * (k % 2) + 8]
        flat[8 * k : 8 * k + 8, :] = pltpu.roll(part, 128 - 16 * (k // 2), 1) if k > 1 else part
    for kx in range(3):
        for ky in range(3):
            for kz in range(3):
                row = (2 - ky) * 40 + kz * 12 + kx * 4
                g1v[kx, ky, kz] = flat[row : row + 4, 0:16]
    for c in stores[2:]:
        c.start()
    for c in stores:
        c.wait()


def solution(mesh):
    sizes = (space_grid(mesh.shape["space"]), mesh.shape["batch"])

    def body(volumes, first_kernel, second_kernel, cotangent):
        cells = math.prod(volumes.shape) // volumes.shape[1] * mesh.size
        scales = (1.0 / math.sqrt(cells), 1.0 / math.sqrt(cells / 8))
        w1 = jnp.transpose(first_kernel, (2, 3, 4, 1, 0))
        w2 = jnp.transpose(second_kernel, (2, 3, 4, 1, 0))
        hbm = pl.BlockSpec(memory_space=pltpu.HBM)
        g1 = sizes[0][0] * sizes[0][2]
        g2 = sizes[0][1] * sizes[1]
        vmem_limit = 60 * 1024 * 1024
        act, pooled_grad, sums1, sums2 = pl.pallas_call(
            functools.partial(kernel, sizes),
            out_shape=(
                jax.ShapeDtypeStruct((2, 32, 2, 8, 128), BF16),
                jax.ShapeDtypeStruct((2, 16, 2, 8, 128), BF16),
                jax.ShapeDtypeStruct((16, 128), F32),
                jax.ShapeDtypeStruct((128, 128), F32),
            ),
            in_specs=[hbm] * 4,
            out_specs=(hbm, hbm, pl.BlockSpec(memory_space=pltpu.VMEM), pl.BlockSpec(memory_space=pltpu.VMEM)),
            scratch_shapes=[
                pltpu.VMEM((2, 6, 4, 16, 256), BF16),
                pltpu.VMEM((2, 384, 128), F32),
                pltpu.VMEM((2, 1456, 256), BF16),
                pltpu.VMEM((2, 1024, 256), F32),
                pltpu.VMEM((2, 8, 2, 16, 128), BF16),
                pltpu.VMEM((2, 2, 8, 2, 16, 128), BF16),
                pltpu.VMEM((2, 2912, 128), BF16),
                pltpu.VMEM((2, 32, 2, 8, 128), BF16),
                pltpu.VMEM((2, 2, 32, 8, 128), BF16),
                pltpu.VMEM((4, 256, 128), F32),
                pltpu.VMEM((512, 128), F32),
                pltpu.VMEM((2, 32, 2, 8, 128), BF16),
                pltpu.VMEM((2, 10, 64, 128), BF16),
                pltpu.VMEM((2, 18, 64, 256), BF16),
                pltpu.VMEM((2, 3072, 128), BF16),
                pltpu.VMEM((256, 128), F32),
                pltpu.VMEM((2, 16, 2, 8, 128), BF16),
                pltpu.VMEM((3, 3, 3, 4, 16), BF16),
                pltpu.VMEM((3, 3, 3, 16, 32), BF16),
                pltpu.VMEM((256, 128), F32),
                pltpu.VMEM((896, 128), F32),
                pltpu.VMEM((432, 128), F32),
                pltpu.VMEM((64, 256), BF16),
                pltpu.VMEM((128, 896), BF16),
                pltpu.VMEM((96, 384), BF16),
                pltpu.VMEM((80, 256), F32),
                pltpu.VMEM((192, 256), F32),
                pltpu.VMEM((16, 8, 128), F32),
                pltpu.VMEM((g1, 16, 128), F32),
                pltpu.VMEM((g2, 16, 128), F32),
                pltpu.VMEM((g1, 16 // g1, 8, 128), F32),
                pltpu.VMEM((g2, 16 // g1, 8, 128), F32),
                pltpu.VMEM((g1, 16 // g1, 8, 128), F32),
                pltpu.SemaphoreType.DMA((15,)),
                pltpu.SemaphoreType.DMA((6, 2)),
                pltpu.SemaphoreType.DMA((6, 2)),
                pltpu.SemaphoreType.DMA((5, max(g1, g2))),
                pltpu.SemaphoreType.DMA((5, max(g1, g2))),
            ],
            compiler_params=pltpu.CompilerParams(
                collective_id=0, has_side_effects=True, vmem_limit_bytes=vmem_limit
            ),
        )(volumes, w1, w2, cotangent)
        act, pooled_grad, grad1, grad2 = pl.pallas_call(
            functools.partial(finish, scales),
            out_shape=(
                jax.ShapeDtypeStruct((2, 32, 2, 8, 128), BF16),
                jax.ShapeDtypeStruct((2, 16, 2, 8, 128), BF16),
                jax.ShapeDtypeStruct((3, 3, 3, 4, 16), F32),
                jax.ShapeDtypeStruct((3, 3, 3, 16, 32), F32),
            ),
            in_specs=[hbm] * 4,
            out_specs=(hbm,) * 4,
            scratch_shapes=[
                pltpu.VMEM((2, 32, 2, 8, 128), BF16),
                pltpu.VMEM((2, 16, 2, 8, 128), BF16),
                pltpu.VMEM((16, 128), F32),
                pltpu.VMEM((128, 128), F32),
                pltpu.VMEM((128, 128), F32),
                pltpu.VMEM((3, 3, 3, 4, 16), F32),
                pltpu.VMEM((3, 3, 3, 16, 32), F32),
                pltpu.SemaphoreType.DMA((8,)),
            ],
            compiler_params=pltpu.CompilerParams(vmem_limit_bytes=vmem_limit),
        )(act, pooled_grad, sums1, sums2)
        return (
            act,
            pooled_grad,
            jnp.transpose(grad1, (4, 3, 0, 1, 2)),
            jnp.transpose(grad2, (4, 3, 0, 1, 2)),
        )

    return jax.shard_map(
        body,
        mesh=mesh,
        in_specs=(
            P("batch", None, "space", None, None),
            P(),
            P(),
            P("batch", None, "space", None, None),
        ),
        out_specs=(
            P("batch", None, "space", None, None),
            P("batch", None, "space", None, None),
            P(),
            P(),
        ),
        check_vma=False,
    )
```

```python
import functools
import math

import jax
import jax.numpy as jnp
from jax import lax
from jax.experimental import pallas as pl
from jax.experimental.pallas import tpu as pltpu
from jax.sharding import PartitionSpec as P

F32 = jnp.float32
BF16 = jnp.bfloat16
MESH = pl.DeviceIdType.MESH


def space_grid(count):
    side = round(count ** (1 / 3))
    if side**3 == count:
        return side, side, side
    return 2, 1, count // 2


def dot(a, b):
    return jnp.dot(a, b, preferred_element_type=F32)


def dot_nt(a, b):
    return lax.dot_general(a, b, (((1,), (1,)), ((), ())), preferred_element_type=F32)


def shifts(v):
    lanes = lax.broadcasted_iota(jnp.int32, v.shape, 1)
    width = v.shape[1]
    before = jnp.where(lanes == 0, 0.0, pltpu.roll(v, 1, 1))
    after = jnp.where(lanes == width - 1, 0.0, pltpu.roll(v, width - 1, 1))
    return before, after


def pair_sums(v):
    first, second = v[:, 0:128], v[:, 128:256]
    lanes = lax.broadcasted_iota(jnp.int32, first.shape, 1)
    mixed = jnp.where(
        (lanes & 1) == 0, first + pltpu.roll(first, 127, 1), second + pltpu.roll(second, 1, 1)
    )
    source = jnp.where(lanes < 64, 2 * lanes, 2 * lanes - 127)
    return jnp.take_along_axis(mixed, source, axis=1)


def doubled(v):
    lanes = lax.broadcasted_iota(jnp.int32, v.shape, 1)
    half = lanes >> 1
    return [jnp.take_along_axis(v, half, axis=1), jnp.take_along_axis(v, half + 64, axis=1)]


def act_and_slope(z):
    t = jnp.tanh(0.5 * z)
    a = 0.65 + 0.35 * t
    return z * a, a + (0.175 * z) * (1.0 - t * t)


def kernel(
    sizes, vol, w1_hbm, w2_hbm, cot, out_act, out_pg, out_s1, out_s2,
    vbuf, vf, u1, slope, pb, ph, u2, cotb, cotf, actf, db, fd, u3, bko, kb, kh, bkf,
    w1, w2, a1s, a2s, w2f, a1, a2, a3, acc1, acc2, pack2, p1, pairs, q1, r1, r2, res,
    local_sem, halo_send, halo_recv, sum_send, sum_recv,
):
    (nx, nzh, ny), nb = sizes
    n_space = nx * nzh * ny
    g1, g2 = nx * ny, nzh * nb
    tp = 16 // g1
    sp, bt = lax.axis_index("space"), lax.axis_index("batch")
    xi = lax.div(sp, nzh * ny)
    zi = lax.rem(lax.div(sp, ny), nzh)
    yi = lax.rem(sp, ny)
    i1 = xi * ny + yi
    i2 = zi * nb + bt
    core = lax.rem(bt, 2)
    zlow = lax.div(bt, 2)
    iz = zi * (nb // 2) + zlow
    right = lax.rem(sp + 1, n_space)
    left = lax.rem(sp + n_space - 1, n_space)

    def peer1(p):
        return (lax.div(p, ny) * (nzh * ny) + zi * ny + lax.rem(p, ny), bt)

    def peer2(p):
        return (xi * (nzh * ny) + lax.div(p, nb) * ny + yi, lax.rem(p, nb))

    def peerz(p):
        low = nb // 2
        return (xi * (nzh * ny) + lax.div(p, low) * ny + yi, lax.rem(p, low) * 2 + core)

    def peerc(p):
        return (sp, zlow * 2 + p)

    barrier = pltpu.get_barrier_semaphore()
    for side in (left, right):
        pl.semaphore_signal(barrier, inc=1, device_id=(side, bt), device_id_type=MESH)

    def greet1(d, c):
        pl.semaphore_signal(barrier, inc=1, device_id=peer1(lax.rem(i1 + d, g1)), device_id_type=MESH)
        return c

    def greet2(d, c):
        pl.semaphore_signal(barrier, inc=1, device_id=peer2(lax.rem(i2 + d, g2)), device_id_type=MESH)
        return c

    lax.fori_loop(1, g1, greet1, 0)
    lax.fori_loop(1, g2, greet2, 0)

    own = []
    for s in range(2):
        for x in range(4):
            own.append(pltpu.make_async_copy(vol.at[s, :, x], vbuf.at[s, x + 1], local_sem.at[s * 4 + x]))
    own.append(pltpu.make_async_copy(cot, cotb, local_sem.at[8]))
    own.append(pltpu.make_async_copy(w1_hbm, w1, local_sem.at[9]))
    own.append(pltpu.make_async_copy(w2_hbm, w2, local_sem.at[10]))
    for c in own:
        c.start()
    for c in own[0:8]:
        c.wait()

    pl.semaphore_wait(barrier, 2 + g1 - 1 + g2 - 1)

    def both_ways(k, to_right, land_right, to_left, land_left):
        one = pltpu.make_async_remote_copy(
            src_ref=to_right, dst_ref=land_right, send_sem=halo_send.at[k, 0], recv_sem=halo_recv.at[k, 0],
            device_id=(right, bt), device_id_type=MESH,
        )
        two = pltpu.make_async_remote_copy(
            src_ref=to_left, dst_ref=land_left, send_sem=halo_send.at[k, 1], recv_sem=halo_recv.at[k, 1],
            device_id=(left, bt), device_id_type=MESH,
        )
        return one, two

    halos = [both_ways(s, vbuf.at[s, 4], vbuf.at[s, 0], vbuf.at[s, 1], vbuf.at[s, 5]) for s in range(2)]
    for pair in halos:
        for c in pair:
            c.start()
    for c in own[8:]:
        c.wait()

    def arrive(pair, low, high):
        for c in pair:
            c.wait()

        @pl.when(sp == 0)
        def _():
            low[...] = jnp.zeros_like(low)

        @pl.when(sp == n_space - 1)
        def _():
            high[...] = jnp.zeros_like(high)

    a1s[...] = jnp.zeros_like(a1s)
    for kx in range(3):
        for ky in range(3):
            for kz in range(3):
                row = ky * 80 + kz * 24 + kx * 4
                a1s[row : row + 4, 0:16] = w1[kx, ky, kz].astype(F32)
    base = a1s[...]
    t1 = base
    for x in range(1, 4):
        t1 = t1 + pltpu.roll(pltpu.roll(base, 4 * x, 0), 16 * x, 1)
    a1[...] = t1.T[0:64].astype(BF16)

    w2f[...] = jnp.zeros_like(w2f)
    w2f[:, 0:32] = w2[...].reshape(432, 32).astype(F32)
    a2s[...] = jnp.zeros_like(a2s)
    for ky in range(3):
        for kx in range(3):
            a2s[ky, kx * 48 : kx * 48 + 48, :] = w2f[(kx * 3 + ky) * 48 : (kx * 3 + ky) * 48 + 48, :]
        base = a2s[ky]
        both = (base + pltpu.roll(pltpu.roll(base, 48, 0), 32, 1)).T[0:64, 0:192].astype(BF16)
        a2[64 * ky : 64 * ky + 64, :] = both
    for ky in range(3):
        pieces = []
        for kz in range(3):
            rows = [((kx * 3 + 2 - ky) * 3 + 2 - kz) * 16 for kx in range(3)]
            zero = jnp.zeros((16, 128), F32)
            kept = [w2f[r : r + 16, :] for r in rows] + [zero]
            both = jnp.concatenate(kept, axis=0) + pltpu.roll(jnp.concatenate([zero] + kept[0:3], axis=0), 32, 1)
            pieces.append(both)
        a3[64 * ky : 64 * ky + 64, 0:128] = (pieces[0] + pltpu.roll(pieces[1], 64, 1)).astype(BF16)
        a3[64 * ky : 64 * ky + 64, 128:192] = pieces[2][:, 0:64].astype(BF16)

    for s in range(2):
        u1[s, 0:80, :] = jnp.zeros((80, 256), BF16)
        u1[s, 1360:1456, :] = jnp.zeros((96, 256), BF16)
        for y in (0, 9):
            db[s, y] = jnp.zeros((64, 128), BF16)
        for y in (0, 17):
            fd[s, y] = jnp.zeros((64, 256), BF16)

    def stage1(s):
        arrive(halos[s], vbuf.at[s, 0], vbuf.at[s, 5])
        planes = vbuf[s].reshape(384, 256).astype(F32)
        for half in range(2):
            vf[half] = planes[:, 128 * half : 128 * half + 128]
        for y in range(16):
            v = jnp.concatenate([vf[half, pl.ds(y, 24, stride=16), :] for half in range(2)], axis=1)
            before, after = shifts(v)
            rows = jnp.concatenate([before, v, after, jnp.zeros((8, 256), F32)], axis=0)
            u1[s, (y + 1) * 80 : (y + 2) * 80, :] = rows.astype(BF16)
        for j in range(8):
            total = None
            for i in range(2):
                y = 2 * j + i
                pre = dot(a1[...], u1[s, y * 80 : y * 80 + 256, :])
                act, sl = act_and_slope(pre)
                slope[s, y * 64 : y * 64 + 64, :] = 0.125 * sl
                total = act if total is None else total + act
            pairs = jnp.concatenate([total[0:16] + total[16:32], total[32:48] + total[48:64]], axis=0)
            pooled = (0.125 * pair_sums(pairs)).astype(BF16)
            for x in range(2):
                pb[s, x, j] = pooled[16 * x : 16 * x + 16]
            mid = pooled.astype(F32)
            before, after = shifts(mid)
            for x in range(2):
                part = slice(16 * x, 16 * x + 16)
                rows = jnp.concatenate([before[part], mid[part], after[part]], axis=0)
                at = j * 192 + (x + 1) * 48
                u2[s, at : at + 48, :] = rows.astype(BF16)
        near = both_ways(2 + s, pb.at[s, 1], ph.at[s, 0], pb.at[s, 0], ph.at[s, 1])
        for c in near:
            c.start()
        return near

    def convolved(matrix, field, count):
        parts = []
        for j in range(4):
            part = dot(matrix, jnp.concatenate([field[2 * j], field[2 * j + 1]], axis=1))
            parts += [part[:, 0:128], part[:, 128:256]]
        out = []
        for j in range(8):
            pre = parts[j][count : 2 * count]
            if j > 0:
                pre = pre + parts[j - 1][0:count]
            if j < 7:
                pre = pre + parts[j + 1][2 * count : 3 * count]
            out.append(pre)
        return out

    def second_layer(s, near):
        for x in range(2):
            cotf[x] = cotb[s, :, x].reshape(256, 128).astype(F32)
        arrive(near, ph.at[s, 0], ph.at[s, 1])
        for j in range(8):
            mid = jnp.concatenate([ph[s, 0, j], ph[s, 1, j]], axis=0).astype(F32)
            before, after = shifts(mid)
            for side in range(2):
                part = slice(16 * side, 16 * side + 16)
                rows = jnp.concatenate([before[part], mid[part], after[part]], axis=0)
                u2[s, j * 192 + side * 144 : j * 192 + side * 144 + 48, :] = rows.astype(BF16)
        field = [u2[s, j * 192 : j * 192 + 192, :] for j in range(8)]
        for j, pre in enumerate(convolved(a2[...], field, 64)):
            act, sl = act_and_slope(pre)
            for x in range(2):
                actf[pl.ds(x * 8 + j, 32, stride=16), :] = act[32 * x : 32 * x + 32]
            got = [cotf[x, pl.ds(j, 32, stride=8), :] for x in range(2)]
            delta = (jnp.concatenate(got, axis=0) * sl).astype(BF16)
            db[s, j + 1] = delta
            mid = delta.astype(F32)
            before, after = shifts(mid)
            for kz, rows in enumerate((before, mid, after)):
                u3[s, j * 192 + kz * 64 : j * 192 + kz * 64 + 64, :] = rows.astype(BF16)
        field = [u3[s, j * 192 : j * 192 + 192, :] for j in range(8)]
        for j, back in enumerate(convolved(a3[...], field, 64)):
            kb[s, 0, j] = back[0:16].astype(BF16)
            bko[s, j] = back[16:48]
            kb[s, 1, j] = back[48:64].astype(BF16)
        pair = both_ways(4 + s, kb.at[s, 1], kh.at[s, 0], kb.at[s, 0], kh.at[s, 1])
        for c in pair:
            c.start()
        out_act[s] = actf[...].reshape(32, 2, 8, 128).astype(BF16)
        return pair

    def second_grad(s):
        fields = [u2[s, y * 192 : y * 192 + 192, :] for y in range(8)]
        deltas = [db[s, y : y + 3].reshape(192, 128) for y in range(8)]
        return dot_nt(jnp.concatenate(fields, axis=1), jnp.concatenate(deltas, axis=1))

    def stage3(s, pair):
        arrive(pair, kh.at[s, 0], kh.at[s, 1])
        for j in range(8):
            back = bko[s, j] + jnp.concatenate([kh[s, 0, j], kh[s, 1, j]], axis=0).astype(F32)
            for x in range(2):
                bkf[pl.ds(x * 8 + j, 16, stride=16), :] = back[16 * x : 16 * x + 16]
            up = jnp.concatenate(doubled(back), axis=1)
            up = jnp.concatenate([up[0:16], up[0:16], up[16:32], up[16:32]], axis=0)
            for y in (2 * j, 2 * j + 1):
                fd[s, y + 1] = (up * slope[s, y * 64 : y * 64 + 64, :]).astype(BF16)
        out_pg[s] = bkf[...].reshape(16, 2, 8, 128).astype(BF16)

    def first_grad(s):
        total = None
        for k in range(4):
            ys = range(4 * k, 4 * k + 4)
            fields = [u1[s, (y + 1) * 80 : (y + 2) * 80, :] for y in ys]
            deltas = [fd[s, y : y + 3].reshape(192, 256) for y in ys]
            part = dot_nt(jnp.concatenate(deltas, axis=1), jnp.concatenate(fields, axis=1))
            total = part if total is None else total + part
        return total

    def exchange(phase, group, index, peer, src, dst):
        def make(d):
            other = lax.rem(index + d, group)
            return pltpu.make_async_remote_copy(
                src_ref=src(other), dst_ref=dst, send_sem=sum_send.at[phase, d], recv_sem=sum_recv.at[phase, d],
                device_id=peer(other), device_id_type=MESH,
            )

        def go(d, c):
            make(d).start()
            return c

        def end(d, c):
            make(d).wait()
            return c

        lax.fori_loop(1, group, go, 0)
        return lambda: lax.fori_loop(1, group, end, 0)

    near = [stage1(0), stage1(1)]
    beside = [second_layer(s, near[s]) for s in range(2)]
    acc2[:, 0:192] = second_grad(0)
    acc2[:, 0:192] += second_grad(1)

    lanes = lax.broadcasted_iota(jnp.int32, (144, 128), 1)
    f2 = None
    for f in range(3):
        ky = 2 - f
        tile = acc2[:, 128 * (f // 2) : 128 * (f // 2) + 128]
        move = 32 * ky - 64 * (f % 2)
        part = pltpu.roll(tile[0:144], move % 128, 1) if move % 128 else tile[0:144]
        part = part + pltpu.roll(tile[48:192], (move - 32) % 128, 1)
        part = jnp.where((lanes >= 32 * ky) & (lanes < 32 * ky + 32), part, 0.0)
        f2 = part if f2 is None else f2 + part
    rest = []
    for ky in range(3):
        part = pltpu.roll(f2[128:144], 96 - 32 * ky, 1)
        rest.append(jnp.where(lanes[0:16] >= 96, part, 0.0))
    rest = jnp.concatenate(rest + [jnp.zeros((80, 128), F32)], axis=0)
    pack2[...] = (f2[0:128] + rest).reshape(16, 8, 128)

    r1[i1] = pack2[pl.ds(i1 * tp, tp)]
    scattered = exchange(0, g1, i1, peer1, lambda p: pack2.at[pl.ds(p * tp, tp)], r1.at[i1])

    acc1[...] = jnp.zeros_like(acc1)
    stage3(0, beside[0])
    acc1[0:192, 0:80] += first_grad(0)
    scattered()
    r2[i2] = jnp.sum(r1[...], axis=0)
    crossed = exchange(1, g2, i2, peer2, lambda p: r2.at[i2], r2.at[i2])
    stage3(1, beside[1])
    acc1[0:192, 0:80] += first_grad(1)

    rows = lax.broadcasted_iota(jnp.int32, (80, 128), 0)
    lanes = lax.broadcasted_iota(jnp.int32, (80, 128), 1)
    folded = []
    turned = acc1[...].T[0:80]
    for half in range(2):
        g = turned[:, 128 * half : 128 * half + 128]
        f1 = g
        for x in range(1, 4):
            f1 = f1 + pltpu.roll(pltpu.roll(g, 80 - 4 * x, 0), 128 - 16 * x, 1)
        f1 = jnp.where((lanes & 63) < 16, f1, 0.0)
        f1c = None
        for kz in range(3):
            part = jnp.where((rows >= 24 * kz) & (rows < 24 * kz + 12), f1, 0.0)
            part = pltpu.roll(part, 80 - 12 * kz, 0) if kz else part
            f1c = part if f1c is None else f1c + part
        folded.append(f1c[0:40])
    packed = [None, None]
    for f in range(3):
        for r in range(5):
            k = f * 5 + r
            part = folded[f // 2][8 * r : 8 * r + 8]
            part = jnp.where((lanes[0:8] >> 6) == f % 2, part, 0.0)
            move = (16 * (k // 2) - 64 * (f % 2)) % 128
            part = pltpu.roll(part, move, 1) if move else part
            packed[k % 2] = part if packed[k % 2] is None else packed[k % 2] + part
    packed = jnp.concatenate(packed, axis=0)
    p1[i1] = packed
    within = exchange(3, g1, i1, peer1, lambda p: p1.at[i1], p1.at[i1])
    within()
    pairs[core] = jnp.sum(p1[...], axis=0)
    exchange(4, 2, core, peerc, lambda p: pairs.at[core], pairs.at[core])()
    q1[iz] = pairs[0] + pairs[1]
    over = exchange(5, g2 // 2, iz, peerz, lambda p: q1.at[iz], q1.at[iz])
    crossed()
    res[i1] = jnp.sum(r2[...], axis=0)
    gathered = exchange(2, g1, i1, peer1, lambda p: res.at[i1], res.at[i1])
    over()
    out_s1[...] = jnp.sum(q1[...], axis=0)
    gathered()
    out_s2[...] = res[...].reshape(128, 128)


def finish(scales, act, pg, sums1, sums2, out_act, out_pg, out_g1, out_g2, flat, g1v, g2v, sem):
    stores = [
        pltpu.make_async_copy(src, dst, sem.at[k])
        for k, (src, dst) in enumerate(((act, out_act), (pg, out_pg), (g2v, out_g2), (g1v, out_g1)))
    ]
    for c in stores[0:2]:
        c.start()
    total = sums2[...] * scales[1]
    rest = pltpu.roll(total[0:48], 32, 1)
    for ky in range(3):
        part = pltpu.roll(total, 128 - 32 * ky, 1) if ky else total
        whole = jnp.concatenate([part, rest[ky * 16 : ky * 16 + 16]], axis=0)[:, 0:32]
        for kx in range(3):
            g2v[kx, ky] = whole[kx * 48 : kx * 48 + 48].reshape(3, 16, 32)
    stores[2].start()
    total = sums1[...] * scales[0]
    for k in range(15):
        part = total[8 * (k % 2) : 8 * (k % 2) + 8]
        flat[8 * k : 8 * k + 8, :] = pltpu.roll(part, 128 - 16 * (k // 2), 1) if k > 1 else part
    for kx in range(3):
        for ky in range(3):
            for kz in range(3):
                row = (2 - ky) * 40 + kz * 12 + kx * 4
                g1v[kx, ky, kz] = flat[row : row + 4, 0:16]
    stores[3].start()
    for c in stores:
        c.wait()


def solution(mesh):
    sizes = (space_grid(mesh.shape["space"]), mesh.shape["batch"])

    def body(volumes, first_kernel, second_kernel, cotangent):
        cells = math.prod(volumes.shape) // volumes.shape[1] * mesh.size
        scales = (1.0 / math.sqrt(cells), 1.0 / math.sqrt(cells / 8))
        w1 = jnp.transpose(first_kernel, (2, 3, 4, 1, 0))
        w2 = jnp.transpose(second_kernel, (2, 3, 4, 1, 0))
        hbm = pl.BlockSpec(memory_space=pltpu.HBM)
        vmem = pl.BlockSpec(memory_space=pltpu.VMEM)
        g1 = sizes[0][0] * sizes[0][2]
        g2 = sizes[0][1] * sizes[1]
        vmem_limit = 63 * 1024 * 1024
        act, pooled_grad, sums1, sums2 = pl.pallas_call(
            functools.partial(kernel, sizes),
            out_shape=(
                pltpu.VMEM((2, 32, 2, 8, 128), BF16),
                pltpu.VMEM((2, 16, 2, 8, 128), BF16),
                pltpu.VMEM((16, 128), F32),
                pltpu.VMEM((128, 128), F32),
            ),
            in_specs=[hbm] * 4,
            out_specs=(vmem,) * 4,
            scratch_shapes=[
                pltpu.VMEM((2, 6, 4, 16, 256), BF16),
                pltpu.VMEM((2, 384, 128), F32),
                pltpu.VMEM((2, 1456, 256), BF16),
                pltpu.VMEM((2, 1024, 256), F32),
                pltpu.VMEM((2, 2, 8, 16, 128), BF16),
                pltpu.VMEM((2, 2, 8, 16, 128), BF16),
                pltpu.VMEM((2, 1536, 128), BF16),
                pltpu.VMEM((2, 32, 2, 8, 128), BF16),
                pltpu.VMEM((2, 256, 128), F32),
                pltpu.VMEM((512, 128), F32),
                pltpu.VMEM((2, 10, 64, 128), BF16),
                pltpu.VMEM((2, 18, 64, 256), BF16),
                pltpu.VMEM((2, 1536, 128), BF16),
                pltpu.VMEM((2, 8, 32, 128), F32),
                pltpu.VMEM((2, 2, 8, 16, 128), BF16),
                pltpu.VMEM((2, 2, 8, 16, 128), BF16),
                pltpu.VMEM((256, 128), F32),
                pltpu.VMEM((3, 3, 3, 4, 16), BF16),
                pltpu.VMEM((3, 3, 3, 16, 32), BF16),
                pltpu.VMEM((256, 128), F32),
                pltpu.VMEM((3, 256, 128), F32),
                pltpu.VMEM((432, 128), F32),
                pltpu.VMEM((64, 256), BF16),
                pltpu.VMEM((192, 192), BF16),
                pltpu.VMEM((192, 192), BF16),
                pltpu.VMEM((256, 128), F32),
                pltpu.VMEM((192, 256), F32),
                pltpu.VMEM((16, 8, 128), F32),
                pltpu.VMEM((g1, 16, 128), F32),
                pltpu.VMEM((2, 16, 128), F32),
                pltpu.VMEM((g2 // 2, 16, 128), F32),
                pltpu.VMEM((g1, 16 // g1, 8, 128), F32),
                pltpu.VMEM((g2, 16 // g1, 8, 128), F32),
                pltpu.VMEM((g1, 16 // g1, 8, 128), F32),
                pltpu.SemaphoreType.DMA((11,)),
                pltpu.SemaphoreType.DMA((6, 2)),
                pltpu.SemaphoreType.DMA((6, 2)),
                pltpu.SemaphoreType.DMA((6, max(g1, g2))),
                pltpu.SemaphoreType.DMA((6, max(g1, g2))),
            ],
            compiler_params=pltpu.CompilerParams(
                collective_id=0, has_side_effects=True, vmem_limit_bytes=vmem_limit
            ),
        )(volumes, w1, w2, cotangent)
        act, pooled_grad, grad1, grad2 = pl.pallas_call(
            functools.partial(finish, scales),
            out_shape=(
                jax.ShapeDtypeStruct((2, 32, 2, 8, 128), BF16),
                jax.ShapeDtypeStruct((2, 16, 2, 8, 128), BF16),
                jax.ShapeDtypeStruct((3, 3, 3, 4, 16), F32),
                jax.ShapeDtypeStruct((3, 3, 3, 16, 32), F32),
            ),
            in_specs=[vmem] * 4,
            out_specs=(hbm,) * 4,
            scratch_shapes=[
                pltpu.VMEM((128, 128), F32),
                pltpu.VMEM((3, 3, 3, 4, 16), F32),
                pltpu.VMEM((3, 3, 3, 16, 32), F32),
                pltpu.SemaphoreType.DMA((4,)),
            ],
            compiler_params=pltpu.CompilerParams(vmem_limit_bytes=16 * 1024 * 1024),
        )(act, pooled_grad, sums1, sums2)
        return (
            act,
            pooled_grad,
            jnp.transpose(grad1, (4, 3, 0, 1, 2)),
            jnp.transpose(grad2, (4, 3, 0, 1, 2)),
        )

    return jax.shard_map(
        body,
        mesh=mesh,
        in_specs=(
            P("batch", None, "space", None, None),
            P(),
            P(),
            P("batch", None, "space", None, None),
        ),
        out_specs=(
            P("batch", None, "space", None, None),
            P("batch", None, "space", None, None),
            P(),
            P(),
        ),
        check_vma=False,
    )
```

```python
import functools
import math

import jax
import jax.numpy as jnp
from jax import lax
from jax.experimental import pallas as pl
from jax.experimental.pallas import tpu as pltpu
from jax.sharding import PartitionSpec as P

F32 = jnp.float32
BF16 = jnp.bfloat16
MESH = pl.DeviceIdType.MESH


def space_grid(count):
    side = round(count ** (1 / 3))
    if side**3 == count:
        return side, side, side
    return 2, 1, count // 2


def hops(step, count):
    return min(step, count - step)


def offsets(nx, ny, nz, cores):
    steps = [
        (dx, dy, dz, dc) for dx in range(nx) for dy in range(ny) for dz in range(nz) for dc in range(cores)
    ]
    far = lambda d: hops(d[0], nx) + hops(d[1], ny) + hops(d[2], nz) + 0.1 * d[3]
    return sorted(steps[1:], key=far, reverse=True)


def dot(a, b):
    return jnp.dot(a, b, preferred_element_type=F32)


def dot_nt(a, b):
    return lax.dot_general(a, b, (((1,), (1,)), ((), ())), preferred_element_type=F32)


def shifts(v):
    lanes = lax.broadcasted_iota(jnp.int32, v.shape, 1)
    width = v.shape[1]
    before = jnp.where(lanes == 0, 0.0, pltpu.roll(v, 1, 1))
    after = jnp.where(lanes == width - 1, 0.0, pltpu.roll(v, width - 1, 1))
    return before, after


def pair_sums(v):
    first, second = v[:, 0:128], v[:, 128:256]
    lanes = lax.broadcasted_iota(jnp.int32, first.shape, 1)
    mixed = jnp.where(
        (lanes & 1) == 0, first + pltpu.roll(first, 127, 1), second + pltpu.roll(second, 1, 1)
    )
    source = jnp.where(lanes < 64, 2 * lanes, 2 * lanes - 127)
    return jnp.take_along_axis(mixed, source, axis=1)


def doubled(v):
    lanes = lax.broadcasted_iota(jnp.int32, v.shape, 1)
    half = lanes >> 1
    return [jnp.take_along_axis(v, half, axis=1), jnp.take_along_axis(v, half + 64, axis=1)]


def act_and_slope(z):
    t = jnp.tanh(0.5 * z)
    a = 0.65 + 0.35 * t
    return z * a, a + (0.175 * z) * (1.0 - t * t)


def kernel(
    sizes, vol, w1_hbm, w2_hbm, cot, out_act, out_pg, out_s1, out_s2,
    vbuf, vf, u1, slope, pb, ph, u2, cotb, ch, cotf, actf, db, fd, u3, bkf,
    w1, w2, a1s, a2s, w2f, a1, a2, a2h, a3, acc1, acc2, pack2, p1, q1, r1, r2, res,
    local_sem, halo_send, halo_recv, sum_send, sum_recv,
):
    (nx, nzh, ny), nb = sizes
    n_space = nx * nzh * ny
    g1 = nx * ny
    tp = 16 // g1
    sp, bt = lax.axis_index("space"), lax.axis_index("batch")
    xi = lax.div(sp, nzh * ny)
    zi = lax.rem(lax.div(sp, ny), nzh)
    yi = lax.rem(sp, ny)
    i1 = xi * ny + yi
    core = lax.rem(bt, 2)
    nzl = nb // 2
    nz = nzh * nzl
    iz = zi * nzl + lax.div(bt, 2)
    right = lax.rem(sp + 1, n_space)
    left = lax.rem(sp + n_space - 1, n_space)

    def at(step):
        dx, dy, dz, dc = step
        x, y, z, c = lax.rem(xi + dx, nx), lax.rem(yi + dy, ny), lax.rem(iz + dz, nz), lax.rem(core + dc, 2)
        place = (x * (nzh * ny) + lax.div(z, nzl) * ny + y, lax.rem(z, nzl) * 2 + c)
        return place, x * ny + y, c

    slab_group = offsets(nx, ny, 1, 1)
    column = offsets(1, 1, nz, 2)

    barrier = pltpu.get_barrier_semaphore()
    for side in (left, right):
        pl.semaphore_signal(barrier, inc=1, device_id=(side, bt), device_id_type=MESH)

    others = slab_group + column
    for step in others:
        pl.semaphore_signal(barrier, inc=1, device_id=at(step)[0], device_id_type=MESH)

    own = []
    for s in range(2):
        for x in range(4):
            own.append(pltpu.make_async_copy(vol.at[s, :, x], vbuf.at[s, x + 1], local_sem.at[s * 4 + x]))
    for s in range(2):
        for x in range(2):
            own.append(pltpu.make_async_copy(cot.at[s, :, x], cotb.at[s, x], local_sem.at[8 + s * 2 + x]))
    own.append(pltpu.make_async_copy(w1_hbm, w1, local_sem.at[12]))
    own.append(pltpu.make_async_copy(w2_hbm, w2, local_sem.at[13]))
    for c in own:
        c.start()
    for c in own[0:8]:
        c.wait()

    pl.semaphore_wait(barrier, 2 + len(others))

    def both_ways(k, to_right, land_right, to_left, land_left):
        one = pltpu.make_async_remote_copy(
            src_ref=to_right, dst_ref=land_right, send_sem=halo_send.at[k, 0], recv_sem=halo_recv.at[k, 0],
            device_id=(right, bt), device_id_type=MESH,
        )
        two = pltpu.make_async_remote_copy(
            src_ref=to_left, dst_ref=land_left, send_sem=halo_send.at[k, 1], recv_sem=halo_recv.at[k, 1],
            device_id=(left, bt), device_id_type=MESH,
        )
        return one, two

    halos = [both_ways(s, vbuf.at[s, 4], vbuf.at[s, 0], vbuf.at[s, 1], vbuf.at[s, 5]) for s in range(2)]
    for pair in halos:
        for c in pair:
            c.start()
    for c in own[8:]:
        c.wait()
    cot_pairs = [both_ways(6 + s, cotb.at[s, 1], ch.at[s, 0], cotb.at[s, 0], ch.at[s, 1]) for s in range(2)]
    for c in cot_pairs[0]:
        c.start()

    def arrive(pair, low, high):
        for c in pair:
            c.wait()

        @pl.when(sp == 0)
        def _():
            low[...] = jnp.zeros_like(low)

        @pl.when(sp == n_space - 1)
        def _():
            high[...] = jnp.zeros_like(high)

    a1s[...] = jnp.zeros_like(a1s)
    for kx in range(3):
        for ky in range(3):
            for kz in range(3):
                row = ky * 80 + kz * 24 + kx * 4
                a1s[row : row + 4, 0:16] = w1[kx, ky, kz].astype(F32)
    base = a1s[...]
    t1 = base
    for x in range(1, 4):
        t1 = t1 + pltpu.roll(pltpu.roll(base, 4 * x, 0), 16 * x, 1)
    a1[...] = t1.T[0:64].astype(BF16)

    w2f[...] = jnp.zeros_like(w2f)
    w2f[:, 0:32] = w2[...].reshape(432, 32).astype(F32)
    a2s[...] = jnp.zeros_like(a2s)
    for ky in range(3):
        for kx in range(3):
            a2s[ky, kx * 48 : kx * 48 + 48, :] = w2f[(kx * 3 + ky) * 48 : (kx * 3 + ky) * 48 + 48, :]
        base = a2s[ky]
        both = (base + pltpu.roll(pltpu.roll(base, 48, 0), 32, 1)).T[0:64, 0:192].astype(BF16)
        a2[64 * ky : 64 * ky + 64, :] = both
        for x in range(2):
            a2h[x, 32 * ky : 32 * ky + 32, :] = both[32 * x : 32 * x + 32]
    for ky in range(3):
        for kz in range(3):
            rows = [((kx * 3 + 2 - ky) * 3 + 2 - kz) * 16 for kx in range(3)]
            blocks = [w2f[r : r + 16, :] for r in rows]
            first = blocks[2] + pltpu.roll(blocks[1], 32, 1) + pltpu.roll(blocks[0], 64, 1)
            both = jnp.concatenate([first, pltpu.roll(first, 32, 1)], axis=0)
            a3[32 * ky : 32 * ky + 32, kz * 128 : kz * 128 + 128] = both.astype(BF16)

    for s in range(2):
        u1[s, 0:80, :] = jnp.zeros((80, 256), BF16)
        u1[s, 1360:1456, :] = jnp.zeros((96, 256), BF16)
        for y in (0, 9):
            db[s, y] = jnp.zeros((64, 128), BF16)
        for y in (0, 17):
            fd[s, y] = jnp.zeros((64, 256), BF16)

    def stage1(s):
        arrive(halos[s], vbuf.at[s, 0], vbuf.at[s, 5])
        planes = vbuf[s].reshape(384, 256).astype(F32)
        for half in range(2):
            vf[half] = planes[:, 128 * half : 128 * half + 128]
        for y in range(16):
            v = jnp.concatenate([vf[half, pl.ds(y, 24, stride=16), :] for half in range(2)], axis=1)
            before, after = shifts(v)
            rows = jnp.concatenate([before, v, after, jnp.zeros((8, 256), F32)], axis=0)
            u1[s, (y + 1) * 80 : (y + 2) * 80, :] = rows.astype(BF16)
        for j in range(8):
            total = None
            for i in range(2):
                y = 2 * j + i
                pre = dot(a1[...], u1[s, y * 80 : y * 80 + 256, :])
                act, sl = act_and_slope(pre)
                slope[s, y * 64 : y * 64 + 64, :] = 0.125 * sl
                total = act if total is None else total + act
            pairs = jnp.concatenate([total[0:16] + total[16:32], total[32:48] + total[48:64]], axis=0)
            pooled = (0.125 * pair_sums(pairs)).astype(BF16)
            for x in range(2):
                pb[s, x, j] = pooled[16 * x : 16 * x + 16]
            mid = pooled.astype(F32)
            before, after = shifts(mid)
            for x in range(2):
                part = slice(16 * x, 16 * x + 16)
                rows = jnp.concatenate([before[part], mid[part], after[part]], axis=0)
                at = j * 288 + (x + 2) * 48
                u2[s, at : at + 48, :] = rows.astype(BF16)
        near = both_ways(2 + s, pb.at[s, 1], ph.at[s, 0, 1], pb.at[s, 0], ph.at[s, 1, 0])
        far = both_ways(4 + s, pb.at[s, 0], ph.at[s, 0, 0], pb.at[s, 1], ph.at[s, 1, 1])
        for c in near:
            c.start()
        return near, far

    def fill(s, planes):
        for j in range(8):
            mid = jnp.concatenate([ph[s, side, x, j] for side, x, at in planes], axis=0).astype(F32)
            before, after = shifts(mid)
            for k, (side, x, at) in enumerate(planes):
                part = slice(16 * k, 16 * k + 16)
                rows = jnp.concatenate([before[part], mid[part], after[part]], axis=0)
                u2[s, j * 288 + at * 48 : j * 288 + at * 48 + 48, :] = rows.astype(BF16)

    def convolved(s, matrix, first, count):
        parts = []
        for j in range(4):
            both = [u2[s, (2 * j + i) * 288 + first : (2 * j + i) * 288 + first + 192, :] for i in range(2)]
            part = dot(matrix, jnp.concatenate(both, axis=1))
            parts += [part[:, 0:128], part[:, 128:256]]
        out = []
        for j in range(8):
            pre = parts[j][count : 2 * count]
            if j > 0:
                pre = pre + parts[j - 1][0:count]
            if j < 7:
                pre = pre + parts[j + 1][2 * count : 3 * count]
            out.append(pre)
        return out

    def spread_delta(s, j, delta, places):
        mid = delta.astype(F32)
        before, after = shifts(mid)
        for kz, rows in enumerate((before, mid, after)):
            rows = rows.astype(BF16)
            for first, count, at in places:
                low = j * 384 + kz * 128 + at
                u3[s, low : low + count, :] = rows[first : first + count]

    def second_own(s, near):
        for x in range(2):
            cotf[x + 1] = cotb[s, x].reshape(256, 128).astype(F32)
        arrive(near, ph.at[s, 0, 1], ph.at[s, 1, 0])
        fill(s, ((0, 1, 1), (1, 0, 4)))
        for j, pre in enumerate(convolved(s, a2[...], 48, 64)):
            act, sl = act_and_slope(pre)
            for x in range(2):
                actf[pl.ds(x * 8 + j, 32, stride=16), :] = act[32 * x : 32 * x + 32]
            got = [cotf[1 + x, pl.ds(j, 32, stride=8), :] for x in range(2)]
            delta = (jnp.concatenate(got, axis=0) * sl).astype(BF16)
            db[s, j + 1] = delta
            spread_delta(s, j, delta, ((0, 64, 32),))
        out_act[s] = actf[...].reshape(32, 2, 8, 128).astype(BF16)

    def second_beside(s, far):
        arrive(cot_pairs[s], ch.at[s, 0], ch.at[s, 1])
        for side in range(2):
            cotf[3 * side] = ch[s, side].reshape(256, 128).astype(F32)
        arrive(far, ph.at[s, 0, 0], ph.at[s, 1, 1])
        fill(s, ((0, 0, 0), (1, 1, 5)))
        low = convolved(s, a2h[0], 0, 32)
        high = convolved(s, a2h[1], 96, 32)
        for j in range(8):
            sl = act_and_slope(jnp.concatenate([low[j], high[j]], axis=0))[1]
            got = [cotf[3 * side, pl.ds(j, 32, stride=8), :] for side in range(2)]
            delta = (jnp.concatenate(got, axis=0) * sl).astype(BF16)
            spread_delta(s, j, delta, ((0, 32, 0), (32, 32, 96)))

    def second_grad(s):
        fields = [u2[s, y * 288 + 48 : y * 288 + 240, :] for y in range(8)]
        deltas = [db[s, y : y + 3].reshape(192, 128) for y in range(8)]
        return dot_nt(jnp.concatenate(fields, axis=1), jnp.concatenate(deltas, axis=1))

    def stage3(s):
        parts = []
        for j in range(4):
            both = jnp.concatenate([u3[s, (2 * j + i) * 384 : (2 * j + i) * 384 + 384, :] for i in range(2)], axis=1)
            part = dot(a3[...], both)
            parts += [part[:, 0:128], part[:, 128:256]]
        for j in range(8):
            back = parts[j][32:64]
            if j > 0:
                back = back + parts[j - 1][0:32]
            if j < 7:
                back = back + parts[j + 1][64:96]
            for x in range(2):
                bkf[pl.ds(x * 8 + j, 16, stride=16), :] = back[16 * x : 16 * x + 16]
            up = jnp.concatenate(doubled(back), axis=1)
            up = jnp.concatenate([up[0:16], up[0:16], up[16:32], up[16:32]], axis=0)
            for y in (2 * j, 2 * j + 1):
                fd[s, y + 1] = (up * slope[s, y * 64 : y * 64 + 64, :]).astype(BF16)
        out_pg[s] = bkf[...].reshape(16, 2, 8, 128).astype(BF16)

    def first_grad(s):
        total = None
        for k in range(4):
            ys = range(4 * k, 4 * k + 4)
            fields = [u1[s, (y + 1) * 80 : (y + 2) * 80, :] for y in ys]
            deltas = [fd[s, y : y + 3].reshape(192, 256) for y in ys]
            part = dot_nt(jnp.concatenate(deltas, axis=1), jnp.concatenate(fields, axis=1))
            total = part if total is None else total + part
        return total

    def exchange(phase, group, src, dst):
        sent = []
        for k, step in enumerate(group):
            place, slab, c = at(step)
            copy = pltpu.make_async_remote_copy(
                src_ref=src(slab, c), dst_ref=dst, send_sem=sum_send.at[phase, k], recv_sem=sum_recv.at[phase, k],
                device_id=place, device_id_type=MESH,
            )
            copy.start()
            sent.append(copy)

        def finished():
            for copy in sent:
                copy.wait()

        return finished

    halves = [stage1(0), stage1(1)]
    for c in (*halves[0][1], *cot_pairs[1], *halves[1][1]):
        c.start()
    second_own(0, halves[0][0])
    acc2[:, 0:192] = second_grad(0)
    second_own(1, halves[1][0])
    acc2[:, 0:192] += second_grad(1)

    lanes = lax.broadcasted_iota(jnp.int32, (144, 128), 1)
    f2 = None
    for f in range(3):
        ky = 2 - f
        tile = acc2[:, 128 * (f // 2) : 128 * (f // 2) + 128]
        move = 32 * ky - 64 * (f % 2)
        part = pltpu.roll(tile[0:144], move % 128, 1) if move % 128 else tile[0:144]
        part = part + pltpu.roll(tile[48:192], (move - 32) % 128, 1)
        part = jnp.where((lanes >= 32 * ky) & (lanes < 32 * ky + 32), part, 0.0)
        f2 = part if f2 is None else f2 + part
    rest = []
    for ky in range(3):
        part = pltpu.roll(f2[128:144], 96 - 32 * ky, 1)
        rest.append(jnp.where(lanes[0:16] >= 96, part, 0.0))
    rest = jnp.concatenate(rest + [jnp.zeros((80, 128), F32)], axis=0)
    pack2[...] = (f2[0:128] + rest).reshape(16, 8, 128)

    r1[i1] = pack2[pl.ds(i1 * tp, tp)]
    scattered = exchange(0, slab_group, lambda slab, c: pack2.at[pl.ds(slab * tp, tp)], r1.at[i1])

    acc1[...] = jnp.zeros_like(acc1)
    for s in range(2):
        second_beside(s, halves[s][1])
        stage3(s)
        acc1[0:192, 0:80] += first_grad(s)

    rows = lax.broadcasted_iota(jnp.int32, (80, 128), 0)
    lanes = lax.broadcasted_iota(jnp.int32, (80, 128), 1)
    folded = []
    turned = acc1[...].T[0:80]
    for half in range(2):
        g = turned[:, 128 * half : 128 * half + 128]
        f1 = g
        for x in range(1, 4):
            f1 = f1 + pltpu.roll(pltpu.roll(g, 80 - 4 * x, 0), 128 - 16 * x, 1)
        f1 = jnp.where((lanes & 63) < 16, f1, 0.0)
        f1c = None
        for kz in range(3):
            part = jnp.where((rows >= 24 * kz) & (rows < 24 * kz + 12), f1, 0.0)
            part = pltpu.roll(part, 80 - 12 * kz, 0) if kz else part
            f1c = part if f1c is None else f1c + part
        folded.append(f1c[0:40])
    packed = [None, None]
    for f in range(3):
        for r in range(5):
            k = f * 5 + r
            part = folded[f // 2][8 * r : 8 * r + 8]
            part = jnp.where((lanes[0:8] >> 6) == f % 2, part, 0.0)
            move = (16 * (k // 2) - 64 * (f % 2)) % 128
            part = pltpu.roll(part, move, 1) if move else part
            packed[k % 2] = part if packed[k % 2] is None else packed[k % 2] + part
    packed = jnp.concatenate(packed, axis=0)
    p1[i1] = packed
    within = exchange(3, slab_group, lambda slab, c: p1.at[i1], p1.at[i1])
    scattered()
    r2[iz * 2 + core] = jnp.sum(r1[...], axis=0)
    crossed = exchange(1, column, lambda slab, c: r2.at[iz * 2 + core], r2.at[iz * 2 + core])
    within()
    q1[iz * 2 + core] = jnp.sum(p1[...], axis=0)
    over = exchange(4, column, lambda slab, c: q1.at[iz * 2 + core], q1.at[iz * 2 + core])
    crossed()
    res[i1] = jnp.sum(r2[...], axis=0)
    gathered = exchange(2, slab_group, lambda slab, c: res.at[i1], res.at[i1])
    over()
    out_s1[...] = jnp.sum(q1[...], axis=0)
    gathered()
    out_s2[...] = res[...].reshape(128, 128)


def finish(scales, act, pg, sums1, sums2, out_act, out_pg, out_g1, out_g2, flat, g1v, g2v, sem):
    stores = [
        pltpu.make_async_copy(src, dst, sem.at[k])
        for k, (src, dst) in enumerate(((act, out_act), (pg, out_pg), (g2v, out_g2), (g1v, out_g1)))
    ]
    for c in stores[0:2]:
        c.start()
    total = sums2[...] * scales[1]
    rest = pltpu.roll(total[0:48], 32, 1)
    for ky in range(3):
        part = pltpu.roll(total, 128 - 32 * ky, 1) if ky else total
        whole = jnp.concatenate([part, rest[ky * 16 : ky * 16 + 16]], axis=0)[:, 0:32]
        for kx in range(3):
            g2v[kx, ky] = whole[kx * 48 : kx * 48 + 48].reshape(3, 16, 32)
    stores[2].start()
    total = sums1[...] * scales[0]
    for k in range(15):
        part = total[8 * (k % 2) : 8 * (k % 2) + 8]
        flat[8 * k : 8 * k + 8, :] = pltpu.roll(part, 128 - 16 * (k // 2), 1) if k > 1 else part
    for kx in range(3):
        for ky in range(3):
            for kz in range(3):
                row = (2 - ky) * 40 + kz * 12 + kx * 4
                g1v[kx, ky, kz] = flat[row : row + 4, 0:16]
    stores[3].start()
    for c in stores:
        c.wait()


def solution(mesh):
    sizes = (space_grid(mesh.shape["space"]), mesh.shape["batch"])

    def body(volumes, first_kernel, second_kernel, cotangent):
        cells = math.prod(volumes.shape) // volumes.shape[1] * mesh.size
        scales = (1.0 / math.sqrt(cells), 1.0 / math.sqrt(cells / 8))
        w1 = jnp.transpose(first_kernel, (2, 3, 4, 1, 0))
        w2 = jnp.transpose(second_kernel, (2, 3, 4, 1, 0))
        hbm = pl.BlockSpec(memory_space=pltpu.HBM)
        vmem = pl.BlockSpec(memory_space=pltpu.VMEM)
        g1 = sizes[0][0] * sizes[0][2]
        g2 = sizes[0][1] * sizes[1]
        vmem_limit = 63 * 1024 * 1024
        act, pooled_grad, sums1, sums2 = pl.pallas_call(
            functools.partial(kernel, sizes),
            out_shape=(
                pltpu.VMEM((2, 32, 2, 8, 128), BF16),
                pltpu.VMEM((2, 16, 2, 8, 128), BF16),
                pltpu.VMEM((16, 128), F32),
                pltpu.VMEM((128, 128), F32),
            ),
            in_specs=[hbm] * 4,
            out_specs=(vmem,) * 4,
            scratch_shapes=[
                pltpu.VMEM((2, 6, 4, 16, 256), BF16),
                pltpu.VMEM((2, 384, 128), F32),
                pltpu.VMEM((2, 1456, 256), BF16),
                pltpu.VMEM((2, 1024, 256), F32),
                pltpu.VMEM((2, 2, 8, 16, 128), BF16),
                pltpu.VMEM((2, 2, 2, 8, 16, 128), BF16),
                pltpu.VMEM((2, 2304, 128), BF16),
                pltpu.VMEM((2, 2, 32, 8, 128), BF16),
                pltpu.VMEM((2, 2, 32, 8, 128), BF16),
                pltpu.VMEM((4, 256, 128), F32),
                pltpu.VMEM((512, 128), F32),
                pltpu.VMEM((2, 10, 64, 128), BF16),
                pltpu.VMEM((2, 18, 64, 256), BF16),
                pltpu.VMEM((2, 3072, 128), BF16),
                pltpu.VMEM((256, 128), F32),
                pltpu.VMEM((3, 3, 3, 4, 16), BF16),
                pltpu.VMEM((3, 3, 3, 16, 32), BF16),
                pltpu.VMEM((256, 128), F32),
                pltpu.VMEM((3, 256, 128), F32),
                pltpu.VMEM((432, 128), F32),
                pltpu.VMEM((64, 256), BF16),
                pltpu.VMEM((192, 192), BF16),
                pltpu.VMEM((2, 96, 192), BF16),
                pltpu.VMEM((96, 384), BF16),
                pltpu.VMEM((256, 128), F32),
                pltpu.VMEM((192, 256), F32),
                pltpu.VMEM((16, 8, 128), F32),
                pltpu.VMEM((g1, 16, 128), F32),
                pltpu.VMEM((g2, 16, 128), F32),
                pltpu.VMEM((g1, 16 // g1, 8, 128), F32),
                pltpu.VMEM((g2, 16 // g1, 8, 128), F32),
                pltpu.VMEM((g1, 16 // g1, 8, 128), F32),
                pltpu.SemaphoreType.DMA((14,)),
                pltpu.SemaphoreType.DMA((8, 2)),
                pltpu.SemaphoreType.DMA((8, 2)),
                pltpu.SemaphoreType.DMA((5, max(g1, g2))),
                pltpu.SemaphoreType.DMA((5, max(g1, g2))),
            ],
            compiler_params=pltpu.CompilerParams(
                collective_id=0, has_side_effects=True, vmem_limit_bytes=vmem_limit
            ),
        )(volumes, w1, w2, cotangent)
        act, pooled_grad, grad1, grad2 = pl.pallas_call(
            functools.partial(finish, scales),
            out_shape=(
                jax.ShapeDtypeStruct((2, 32, 2, 8, 128), BF16),
                jax.ShapeDtypeStruct((2, 16, 2, 8, 128), BF16),
                jax.ShapeDtypeStruct((3, 3, 3, 4, 16), F32),
                jax.ShapeDtypeStruct((3, 3, 3, 16, 32), F32),
            ),
            in_specs=[vmem] * 4,
            out_specs=(hbm,) * 4,
            scratch_shapes=[
                pltpu.VMEM((128, 128), F32),
                pltpu.VMEM((3, 3, 3, 4, 16), F32),
                pltpu.VMEM((3, 3, 3, 16, 32), F32),
                pltpu.SemaphoreType.DMA((4,)),
            ],
            compiler_params=pltpu.CompilerParams(vmem_limit_bytes=16 * 1024 * 1024),
        )(act, pooled_grad, sums1, sums2)
        return (
            act,
            pooled_grad,
            jnp.transpose(grad1, (4, 3, 0, 1, 2)),
            jnp.transpose(grad2, (4, 3, 0, 1, 2)),
        )

    return jax.shard_map(
        body,
        mesh=mesh,
        in_specs=(
            P("batch", None, "space", None, None),
            P(),
            P(),
            P("batch", None, "space", None, None),
        ),
        out_specs=(
            P("batch", None, "space", None, None),
            P("batch", None, "space", None, None),
            P(),
            P(),
        ),
        check_vma=False,
    )
```

```python
import functools
import math

import jax
import jax.numpy as jnp
from jax import lax
from jax.experimental import pallas as pl
from jax.experimental.pallas import tpu as pltpu
from jax.sharding import PartitionSpec as P

F32 = jnp.float32
BF16 = jnp.bfloat16
MESH = pl.DeviceIdType.MESH


def space_grid(count):
    side = round(count ** (1 / 3))
    if side**3 == count:
        return side, side, side
    return 2, 1, count // 2


def hops(step, count):
    return min(step, count - step)


def offsets(nx, ny, nz, cores):
    steps = [
        (dx, dy, dz, dc) for dx in range(nx) for dy in range(ny) for dz in range(nz) for dc in range(cores)
    ]
    far = lambda d: hops(d[0], nx) + hops(d[1], ny) + hops(d[2], nz) + 0.1 * d[3]
    return sorted(steps[1:], key=far, reverse=True)


def dot(a, b):
    return jnp.dot(a, b, preferred_element_type=F32)


def dot_nt(a, b):
    return lax.dot_general(a, b, (((1,), (1,)), ((), ())), preferred_element_type=F32)


def shifts(v):
    lanes = lax.broadcasted_iota(jnp.int32, v.shape, 1)
    width = v.shape[1]
    before = jnp.where(lanes == 0, 0.0, pltpu.roll(v, 1, 1))
    after = jnp.where(lanes == width - 1, 0.0, pltpu.roll(v, width - 1, 1))
    return before, after


def pair_sums(v):
    first, second = v[:, 0:128], v[:, 128:256]
    lanes = lax.broadcasted_iota(jnp.int32, first.shape, 1)
    mixed = jnp.where(
        (lanes & 1) == 0, first + pltpu.roll(first, 127, 1), second + pltpu.roll(second, 1, 1)
    )
    source = jnp.where(lanes < 64, 2 * lanes, 2 * lanes - 127)
    return jnp.take_along_axis(mixed, source, axis=1)


def doubled(v):
    lanes = lax.broadcasted_iota(jnp.int32, v.shape, 1)
    half = lanes >> 1
    return [jnp.take_along_axis(v, half, axis=1), jnp.take_along_axis(v, half + 64, axis=1)]


def act_and_slope(z):
    t = jnp.tanh(0.5 * z)
    a = 0.65 + 0.35 * t
    return z * a, a + (0.175 * z) * (1.0 - t * t)


def kernel(
    sizes, vol, w1_hbm, w2_hbm, cot, out_act, out_pg, out_s1, out_s2,
    vbuf, vf, u1, slope, pb, ph, u2, cotb, ch, cotf, actf, db, fd, u3, bkf,
    w1, w2, a1s, a2s, w2f, a1, a2, a2h, a3, acc1, acc2, pack2, p1, q1, r1, r2, res,
    local_sem, halo_send, halo_recv, sum_send, sum_recv,
):
    (nx, nzh, ny), nb = sizes
    n_space = nx * nzh * ny
    g1 = nx * ny
    tp = 16 // g1
    sp, bt = lax.axis_index("space"), lax.axis_index("batch")
    xi = lax.div(sp, nzh * ny)
    zi = lax.rem(lax.div(sp, ny), nzh)
    yi = lax.rem(sp, ny)
    i1 = xi * ny + yi
    core = lax.rem(bt, 2)
    nzl = nb // 2
    nz = nzh * nzl
    iz = zi * nzl + lax.div(bt, 2)
    right = lax.rem(sp + 1, n_space)
    left = lax.rem(sp + n_space - 1, n_space)

    def at(step):
        dx, dy, dz, dc = step
        x, y, z, c = lax.rem(xi + dx, nx), lax.rem(yi + dy, ny), lax.rem(iz + dz, nz), lax.rem(core + dc, 2)
        place = (x * (nzh * ny) + lax.div(z, nzl) * ny + y, lax.rem(z, nzl) * 2 + c)
        return place, x * ny + y, c

    slab_group = offsets(nx, ny, 1, 1)
    column = offsets(1, 1, nz, 2)

    barrier = pltpu.get_barrier_semaphore()
    for side in (left, right):
        pl.semaphore_signal(barrier, inc=1, device_id=(side, bt), device_id_type=MESH)

    others = slab_group + column
    near = lambda d: hops(d[0], nx) + hops(d[1], ny) + hops(d[2], nz) + 0.1 * d[3]
    for step in sorted(others, key=near, reverse=True):
        pl.semaphore_signal(barrier, inc=1, device_id=at(step)[0], device_id_type=MESH)

    own = []
    for s in range(2):
        for x in range(4):
            own.append(pltpu.make_async_copy(vol.at[s, :, x], vbuf.at[s, x + 1], local_sem.at[s * 4 + x]))
    for s in range(2):
        for x in range(2):
            own.append(pltpu.make_async_copy(cot.at[s, :, x], cotb.at[s, x], local_sem.at[8 + s * 2 + x]))
    own.append(pltpu.make_async_copy(w1_hbm, w1, local_sem.at[12]))
    own.append(pltpu.make_async_copy(w2_hbm, w2, local_sem.at[13]))
    for c in own:
        c.start()
    for c in own[0:8]:
        c.wait()

    pl.semaphore_wait(barrier, 2 + len(others))

    def both_ways(k, to_right, land_right, to_left, land_left):
        one = pltpu.make_async_remote_copy(
            src_ref=to_right, dst_ref=land_right, send_sem=halo_send.at[k, 0], recv_sem=halo_recv.at[k, 0],
            device_id=(right, bt), device_id_type=MESH,
        )
        two = pltpu.make_async_remote_copy(
            src_ref=to_left, dst_ref=land_left, send_sem=halo_send.at[k, 1], recv_sem=halo_recv.at[k, 1],
            device_id=(left, bt), device_id_type=MESH,
        )
        return one, two

    halos = [both_ways(s, vbuf.at[s, 4], vbuf.at[s, 0], vbuf.at[s, 1], vbuf.at[s, 5]) for s in range(2)]
    for pair in halos:
        for c in pair:
            c.start()
    for c in own[8:]:
        c.wait()
    cot_pairs = [both_ways(6 + s, cotb.at[s, 1], ch.at[s, 0], cotb.at[s, 0], ch.at[s, 1]) for s in range(2)]

    def arrive(pair, low, high):
        for c in pair:
            c.wait_recv()

        @pl.when(sp == 0)
        def _():
            low[...] = jnp.zeros_like(low)

        @pl.when(sp == n_space - 1)
        def _():
            high[...] = jnp.zeros_like(high)

    a1s[...] = jnp.zeros_like(a1s)
    for kx in range(3):
        for ky in range(3):
            for kz in range(3):
                row = ky * 80 + kz * 24 + kx * 4
                a1s[row : row + 4, 0:16] = w1[kx, ky, kz].astype(F32)
    base = a1s[...]
    t1 = base
    for x in range(1, 4):
        t1 = t1 + pltpu.roll(pltpu.roll(base, 4 * x, 0), 16 * x, 1)
    a1[...] = t1.T[0:64].astype(BF16)

    w2f[...] = jnp.zeros_like(w2f)
    w2f[:, 0:32] = w2[...].reshape(432, 32).astype(F32)
    a2s[...] = jnp.zeros_like(a2s)
    for ky in range(3):
        for kx in range(3):
            a2s[ky, kx * 48 : kx * 48 + 48, :] = w2f[(kx * 3 + ky) * 48 : (kx * 3 + ky) * 48 + 48, :]
        base = a2s[ky]
        both = (base + pltpu.roll(pltpu.roll(base, 48, 0), 32, 1)).T[0:64, 0:192].astype(BF16)
        a2[64 * ky : 64 * ky + 64, :] = both
        for x in range(2):
            a2h[x, 32 * ky : 32 * ky + 32, :] = both[32 * x : 32 * x + 32]
    for ky in range(3):
        for kz in range(3):
            rows = [((kx * 3 + 2 - ky) * 3 + 2 - kz) * 16 for kx in range(3)]
            blocks = [w2f[r : r + 16, :] for r in rows]
            first = blocks[2] + pltpu.roll(blocks[1], 32, 1) + pltpu.roll(blocks[0], 64, 1)
            both = jnp.concatenate([first, pltpu.roll(first, 32, 1)], axis=0)
            a3[32 * ky : 32 * ky + 32, kz * 128 : kz * 128 + 128] = both.astype(BF16)

    for s in range(2):
        u1[s, 0:80, :] = jnp.zeros((80, 256), BF16)
        u1[s, 1360:1456, :] = jnp.zeros((96, 256), BF16)
        for y in (0, 9):
            db[s, y] = jnp.zeros((64, 128), BF16)
        for y in (0, 17):
            fd[s, y] = jnp.zeros((64, 256), BF16)

    def sent_off(*pairs):
        for pair in pairs:
            for c in pair:
                c.wait_send()

    sent_off(*halos)
    for c in (*cot_pairs[0], *cot_pairs[1]):
        c.start()

    def stage1(s):
        arrive(halos[s], vbuf.at[s, 0], vbuf.at[s, 5])
        planes = vbuf[s].reshape(384, 256).astype(F32)
        for half in range(2):
            vf[half] = planes[:, 128 * half : 128 * half + 128]
        for y in range(16):
            v = jnp.concatenate([vf[half, pl.ds(y, 24, stride=16), :] for half in range(2)], axis=1)
            before, after = shifts(v)
            rows = jnp.concatenate([before, v, after, jnp.zeros((8, 256), F32)], axis=0)
            u1[s, (y + 1) * 80 : (y + 2) * 80, :] = rows.astype(BF16)
        for j in range(8):
            total = None
            for i in range(2):
                y = 2 * j + i
                pre = dot(a1[...], u1[s, y * 80 : y * 80 + 256, :])
                act, sl = act_and_slope(pre)
                slope[s, y * 64 : y * 64 + 64, :] = 0.125 * sl
                total = act if total is None else total + act
            pairs = jnp.concatenate([total[0:16] + total[16:32], total[32:48] + total[48:64]], axis=0)
            pooled = (0.125 * pair_sums(pairs)).astype(BF16)
            for x in range(2):
                pb[s, x, j] = pooled[16 * x : 16 * x + 16]
            mid = pooled.astype(F32)
            before, after = shifts(mid)
            for x in range(2):
                part = slice(16 * x, 16 * x + 16)
                rows = jnp.concatenate([before[part], mid[part], after[part]], axis=0)
                at = j * 288 + (x + 2) * 48
                u2[s, at : at + 48, :] = rows.astype(BF16)
        near = both_ways(2 + s, pb.at[s, 1], ph.at[s, 0, 1], pb.at[s, 0], ph.at[s, 1, 0])
        far = both_ways(4 + s, pb.at[s, 0], ph.at[s, 0, 0], pb.at[s, 1], ph.at[s, 1, 1])
        for c in near:
            c.start()
        return near, far

    def fill(s, planes):
        for j in range(8):
            mid = jnp.concatenate([ph[s, side, x, j] for side, x, at in planes], axis=0).astype(F32)
            before, after = shifts(mid)
            for k, (side, x, at) in enumerate(planes):
                part = slice(16 * k, 16 * k + 16)
                rows = jnp.concatenate([before[part], mid[part], after[part]], axis=0)
                u2[s, j * 288 + at * 48 : j * 288 + at * 48 + 48, :] = rows.astype(BF16)

    def convolved(s, matrix, first, count):
        parts = []
        for j in range(4):
            both = [u2[s, (2 * j + i) * 288 + first : (2 * j + i) * 288 + first + 192, :] for i in range(2)]
            part = dot(matrix, jnp.concatenate(both, axis=1))
            parts += [part[:, 0:128], part[:, 128:256]]
        out = []
        for j in range(8):
            pre = parts[j][count : 2 * count]
            if j > 0:
                pre = pre + parts[j - 1][0:count]
            if j < 7:
                pre = pre + parts[j + 1][2 * count : 3 * count]
            out.append(pre)
        return out

    def spread_delta(s, j, delta, places):
        mid = delta.astype(F32)
        before, after = shifts(mid)
        for kz, rows in enumerate((before, mid, after)):
            rows = rows.astype(BF16)
            for first, count, at in places:
                low = j * 384 + kz * 128 + at
                u3[s, low : low + count, :] = rows[first : first + count]

    def second_own(s, near):
        for x in range(2):
            cotf[x + 1] = cotb[s, x].reshape(256, 128).astype(F32)
        arrive(near, ph.at[s, 0, 1], ph.at[s, 1, 0])
        fill(s, ((0, 1, 1), (1, 0, 4)))
        for j, pre in enumerate(convolved(s, a2[...], 48, 64)):
            act, sl = act_and_slope(pre)
            for x in range(2):
                actf[s, pl.ds(x * 8 + j, 32, stride=16), :] = act[32 * x : 32 * x + 32]
            got = [cotf[1 + x, pl.ds(j, 32, stride=8), :] for x in range(2)]
            db[s, j + 1] = (jnp.concatenate(got, axis=0) * sl).astype(BF16)

    def after_own(s):
        out_act[s] = actf[s].reshape(32, 2, 8, 128).astype(BF16)
        for j in range(8):
            spread_delta(s, j, db[s, j + 1], ((0, 64, 32),))

    def second_beside(s, far):
        arrive(cot_pairs[s], ch.at[s, 0], ch.at[s, 1])
        for side in range(2):
            cotf[3 * side] = ch[s, side].reshape(256, 128).astype(F32)
        arrive(far, ph.at[s, 0, 0], ph.at[s, 1, 1])
        fill(s, ((0, 0, 0), (1, 1, 5)))
        low = convolved(s, a2h[0], 0, 32)
        high = convolved(s, a2h[1], 96, 32)
        for j in range(8):
            sl = act_and_slope(jnp.concatenate([low[j], high[j]], axis=0))[1]
            got = [cotf[3 * side, pl.ds(j, 32, stride=8), :] for side in range(2)]
            delta = (jnp.concatenate(got, axis=0) * sl).astype(BF16)
            spread_delta(s, j, delta, ((0, 32, 0), (32, 32, 96)))

    def second_grad(s):
        fields = [u2[s, y * 288 + 48 : y * 288 + 240, :] for y in range(8)]
        deltas = [db[s, y : y + 3].reshape(192, 128) for y in range(8)]
        return dot_nt(jnp.concatenate(fields, axis=1), jnp.concatenate(deltas, axis=1))

    def stage3(s):
        parts = []
        for j in range(4):
            both = jnp.concatenate([u3[s, (2 * j + i) * 384 : (2 * j + i) * 384 + 384, :] for i in range(2)], axis=1)
            part = dot(a3[...], both)
            parts += [part[:, 0:128], part[:, 128:256]]
        for j in range(8):
            back = parts[j][32:64]
            if j > 0:
                back = back + parts[j - 1][0:32]
            if j < 7:
                back = back + parts[j + 1][64:96]
            for x in range(2):
                bkf[pl.ds(x * 8 + j, 16, stride=16), :] = back[16 * x : 16 * x + 16]
            up = jnp.concatenate(doubled(back), axis=1)
            up = jnp.concatenate([up[0:16], up[0:16], up[16:32], up[16:32]], axis=0)
            for y in (2 * j, 2 * j + 1):
                fd[s, y + 1] = (up * slope[s, y * 64 : y * 64 + 64, :]).astype(BF16)
        out_pg[s] = bkf[...].reshape(16, 2, 8, 128).astype(BF16)

    def first_grad(s):
        total = None
        for k in range(4):
            ys = range(4 * k, 4 * k + 4)
            fields = [u1[s, (y + 1) * 80 : (y + 2) * 80, :] for y in ys]
            deltas = [fd[s, y : y + 3].reshape(192, 256) for y in ys]
            part = dot_nt(jnp.concatenate(deltas, axis=1), jnp.concatenate(fields, axis=1))
            total = part if total is None else total + part
        return total

    def exchange(phase, group, src, dst):
        sent = []
        for k, step in enumerate(group):
            place, slab, c = at(step)
            copy = pltpu.make_async_remote_copy(
                src_ref=src(slab, c), dst_ref=dst, send_sem=sum_send.at[phase, k], recv_sem=sum_recv.at[phase, k],
                device_id=place, device_id_type=MESH,
            )
            copy.start()
            sent.append(copy)

        def finished():
            for copy in sent:
                copy.wait()

        return finished

    halves = [stage1(0), stage1(1)]
    for c in (*halves[0][1], *halves[1][1]):
        c.start()
    second_own(0, halves[0][0])
    acc2[:, 0:192] = second_grad(0)
    second_own(1, halves[1][0])
    acc2[:, 0:192] += second_grad(1)

    lanes = lax.broadcasted_iota(jnp.int32, (144, 128), 1)
    f2 = None
    for f in range(3):
        ky = 2 - f
        tile = acc2[:, 128 * (f // 2) : 128 * (f // 2) + 128]
        move = 32 * ky - 64 * (f % 2)
        part = pltpu.roll(tile[0:144], move % 128, 1) if move % 128 else tile[0:144]
        part = part + pltpu.roll(tile[48:192], (move - 32) % 128, 1)
        part = jnp.where((lanes >= 32 * ky) & (lanes < 32 * ky + 32), part, 0.0)
        f2 = part if f2 is None else f2 + part
    rest = []
    for ky in range(3):
        part = pltpu.roll(f2[128:144], 96 - 32 * ky, 1)
        rest.append(jnp.where(lanes[0:16] >= 96, part, 0.0))
    rest = jnp.concatenate(rest + [jnp.zeros((80, 128), F32)], axis=0)
    pack2[...] = (f2[0:128] + rest).reshape(16, 8, 128)

    r1[i1] = pack2[pl.ds(i1 * tp, tp)]
    scattered = exchange(0, slab_group, lambda slab, c: pack2.at[pl.ds(slab * tp, tp)], r1.at[i1])

    acc1[...] = jnp.zeros_like(acc1)
    for s in range(2):
        after_own(s)
    for s in range(2):
        second_beside(s, halves[s][1])
        stage3(s)
        acc1[0:192, 0:80] += first_grad(s)

    rows = lax.broadcasted_iota(jnp.int32, (80, 128), 0)
    lanes = lax.broadcasted_iota(jnp.int32, (80, 128), 1)
    folded = []
    turned = acc1[...].T[0:80]
    for half in range(2):
        g = turned[:, 128 * half : 128 * half + 128]
        f1 = g
        for x in range(1, 4):
            f1 = f1 + pltpu.roll(pltpu.roll(g, 80 - 4 * x, 0), 128 - 16 * x, 1)
        f1 = jnp.where((lanes & 63) < 16, f1, 0.0)
        f1c = None
        for kz in range(3):
            part = jnp.where((rows >= 24 * kz) & (rows < 24 * kz + 12), f1, 0.0)
            part = pltpu.roll(part, 80 - 12 * kz, 0) if kz else part
            f1c = part if f1c is None else f1c + part
        folded.append(f1c[0:40])
    packed = [None, None]
    for f in range(3):
        for r in range(5):
            k = f * 5 + r
            part = folded[f // 2][8 * r : 8 * r + 8]
            part = jnp.where((lanes[0:8] >> 6) == f % 2, part, 0.0)
            move = (16 * (k // 2) - 64 * (f % 2)) % 128
            part = pltpu.roll(part, move, 1) if move else part
            packed[k % 2] = part if packed[k % 2] is None else packed[k % 2] + part
    packed = jnp.concatenate(packed, axis=0)
    p1[i1] = packed
    within = exchange(3, slab_group, lambda slab, c: p1.at[i1], p1.at[i1])
    scattered()
    r2[iz * 2 + core] = jnp.sum(r1[...], axis=0)
    crossed = exchange(1, column, lambda slab, c: r2.at[iz * 2 + core], r2.at[iz * 2 + core])
    within()
    q1[iz * 2 + core] = jnp.sum(p1[...], axis=0)
    over = exchange(4, column, lambda slab, c: q1.at[iz * 2 + core], q1.at[iz * 2 + core])
    crossed()
    res[i1] = jnp.sum(r2[...], axis=0)
    gathered = exchange(2, slab_group, lambda slab, c: res.at[i1], res.at[i1])
    over()
    out_s1[...] = jnp.sum(q1[...], axis=0)
    gathered()
    sent_off(*(h[0] for h in halves), *(h[1] for h in halves), *cot_pairs)
    out_s2[...] = res[...].reshape(128, 128)


def finish(scales, act, pg, sums1, sums2, out_act, out_pg, out_g1, out_g2, flat, g1v, g2v, sem):
    stores = [
        pltpu.make_async_copy(src, dst, sem.at[k])
        for k, (src, dst) in enumerate(((act, out_act), (pg, out_pg), (g2v, out_g2), (g1v, out_g1)))
    ]
    for c in stores[0:2]:
        c.start()
    total = sums2[...] * scales[1]
    rest = pltpu.roll(total[0:48], 32, 1)
    for ky in range(3):
        part = pltpu.roll(total, 128 - 32 * ky, 1) if ky else total
        whole = jnp.concatenate([part, rest[ky * 16 : ky * 16 + 16]], axis=0)[:, 0:32]
        for kx in range(3):
            g2v[kx, ky] = whole[kx * 48 : kx * 48 + 48].reshape(3, 16, 32)
    stores[2].start()
    total = sums1[...] * scales[0]
    for k in range(15):
        part = total[8 * (k % 2) : 8 * (k % 2) + 8]
        flat[8 * k : 8 * k + 8, :] = pltpu.roll(part, 128 - 16 * (k // 2), 1) if k > 1 else part
    for kx in range(3):
        for ky in range(3):
            for kz in range(3):
                row = (2 - ky) * 40 + kz * 12 + kx * 4
                g1v[kx, ky, kz] = flat[row : row + 4, 0:16]
    stores[3].start()
    for c in stores:
        c.wait()


def solution(mesh):
    sizes = (space_grid(mesh.shape["space"]), mesh.shape["batch"])

    def body(volumes, first_kernel, second_kernel, cotangent):
        cells = math.prod(volumes.shape) // volumes.shape[1] * mesh.size
        scales = (1.0 / math.sqrt(cells), 1.0 / math.sqrt(cells / 8))
        w1 = jnp.transpose(first_kernel, (2, 3, 4, 1, 0))
        w2 = jnp.transpose(second_kernel, (2, 3, 4, 1, 0))
        hbm = pl.BlockSpec(memory_space=pltpu.HBM)
        vmem = pl.BlockSpec(memory_space=pltpu.VMEM)
        g1 = sizes[0][0] * sizes[0][2]
        g2 = sizes[0][1] * sizes[1]
        vmem_limit = 63 * 1024 * 1024
        act, pooled_grad, sums1, sums2 = pl.pallas_call(
            functools.partial(kernel, sizes),
            out_shape=(
                pltpu.VMEM((2, 32, 2, 8, 128), BF16),
                pltpu.VMEM((2, 16, 2, 8, 128), BF16),
                pltpu.VMEM((16, 128), F32),
                pltpu.VMEM((128, 128), F32),
            ),
            in_specs=[hbm] * 4,
            out_specs=(vmem,) * 4,
            scratch_shapes=[
                pltpu.VMEM((2, 6, 4, 16, 256), BF16),
                pltpu.VMEM((2, 384, 128), F32),
                pltpu.VMEM((2, 1456, 256), BF16),
                pltpu.VMEM((2, 1024, 256), F32),
                pltpu.VMEM((2, 2, 8, 16, 128), BF16),
                pltpu.VMEM((2, 2, 2, 8, 16, 128), BF16),
                pltpu.VMEM((2, 2304, 128), BF16),
                pltpu.VMEM((2, 2, 32, 8, 128), BF16),
                pltpu.VMEM((2, 2, 32, 8, 128), BF16),
                pltpu.VMEM((4, 256, 128), F32),
                pltpu.VMEM((2, 512, 128), F32),
                pltpu.VMEM((2, 10, 64, 128), BF16),
                pltpu.VMEM((2, 18, 64, 256), BF16),
                pltpu.VMEM((2, 3072, 128), BF16),
                pltpu.VMEM((256, 128), F32),
                pltpu.VMEM((3, 3, 3, 4, 16), BF16),
                pltpu.VMEM((3, 3, 3, 16, 32), BF16),
                pltpu.VMEM((256, 128), F32),
                pltpu.VMEM((3, 256, 128), F32),
                pltpu.VMEM((432, 128), F32),
                pltpu.VMEM((64, 256), BF16),
                pltpu.VMEM((192, 192), BF16),
                pltpu.VMEM((2, 96, 192), BF16),
                pltpu.VMEM((96, 384), BF16),
                pltpu.VMEM((256, 128), F32),
                pltpu.VMEM((192, 256), F32),
                pltpu.VMEM((16, 8, 128), F32),
                pltpu.VMEM((g1, 16, 128), F32),
                pltpu.VMEM((g2, 16, 128), F32),
                pltpu.VMEM((g1, 16 // g1, 8, 128), F32),
                pltpu.VMEM((g2, 16 // g1, 8, 128), F32),
                pltpu.VMEM((g1, 16 // g1, 8, 128), F32),
                pltpu.SemaphoreType.DMA((14,)),
                pltpu.SemaphoreType.DMA((8, 2)),
                pltpu.SemaphoreType.DMA((8, 2)),
                pltpu.SemaphoreType.DMA((5, max(g1, g2))),
                pltpu.SemaphoreType.DMA((5, max(g1, g2))),
            ],
            compiler_params=pltpu.CompilerParams(
                collective_id=0, has_side_effects=True, vmem_limit_bytes=vmem_limit
            ),
        )(volumes, w1, w2, cotangent)
        act, pooled_grad, grad1, grad2 = pl.pallas_call(
            functools.partial(finish, scales),
            out_shape=(
                jax.ShapeDtypeStruct((2, 32, 2, 8, 128), BF16),
                jax.ShapeDtypeStruct((2, 16, 2, 8, 128), BF16),
                jax.ShapeDtypeStruct((3, 3, 3, 4, 16), F32),
                jax.ShapeDtypeStruct((3, 3, 3, 16, 32), F32),
            ),
            in_specs=[vmem] * 4,
            out_specs=(hbm,) * 4,
            scratch_shapes=[
                pltpu.VMEM((128, 128), F32),
                pltpu.VMEM((3, 3, 3, 4, 16), F32),
                pltpu.VMEM((3, 3, 3, 16, 32), F32),
                pltpu.SemaphoreType.DMA((4,)),
            ],
            compiler_params=pltpu.CompilerParams(vmem_limit_bytes=16 * 1024 * 1024),
        )(act, pooled_grad, sums1, sums2)
        return (
            act,
            pooled_grad,
            jnp.transpose(grad1, (4, 3, 0, 1, 2)),
            jnp.transpose(grad2, (4, 3, 0, 1, 2)),
        )

    return jax.shard_map(
        body,
        mesh=mesh,
        in_specs=(
            P("batch", None, "space", None, None),
            P(),
            P(),
            P("batch", None, "space", None, None),
        ),
        out_specs=(
            P("batch", None, "space", None, None),
            P("batch", None, "space", None, None),
            P(),
            P(),
        ),
        check_vma=False,
    )
```

```python
import functools
import math

import jax
import jax.numpy as jnp
from jax import lax
from jax.experimental import pallas as pl
from jax.experimental.pallas import tpu as pltpu
from jax.sharding import PartitionSpec as P

F32 = jnp.float32
BF16 = jnp.bfloat16
MESH = pl.DeviceIdType.MESH


def space_grid(count):
    side = round(count ** (1 / 3))
    if side**3 == count:
        return side, side, side
    return 2, 1, count // 2


def hops(step, count):
    return min(step, count - step)


def offsets(nx, ny, nz, cores):
    steps = [
        (dx, dy, dz, dc) for dx in range(nx) for dy in range(ny) for dz in range(nz) for dc in range(cores)
    ]
    far = lambda d: hops(d[0], nx) + hops(d[1], ny) + hops(d[2], nz) + 0.1 * d[3]
    return sorted(steps[1:], key=far, reverse=True)


def dot(a, b):
    return jnp.dot(a, b, preferred_element_type=F32)


def dot_nt(a, b):
    return lax.dot_general(a, b, (((1,), (1,)), ((), ())), preferred_element_type=F32)


def shifts(v):
    lanes = lax.broadcasted_iota(jnp.int32, v.shape, 1)
    width = v.shape[1]
    before = jnp.where(lanes == 0, 0.0, pltpu.roll(v, 1, 1))
    after = jnp.where(lanes == width - 1, 0.0, pltpu.roll(v, width - 1, 1))
    return before, after


def pair_sums(v):
    first, second = v[:, 0:128], v[:, 128:256]
    lanes = lax.broadcasted_iota(jnp.int32, first.shape, 1)
    mixed = jnp.where(
        (lanes & 1) == 0, first + pltpu.roll(first, 127, 1), second + pltpu.roll(second, 1, 1)
    )
    source = jnp.where(lanes < 64, 2 * lanes, 2 * lanes - 127)
    return jnp.take_along_axis(mixed, source, axis=1)


def doubled(v):
    lanes = lax.broadcasted_iota(jnp.int32, v.shape, 1)
    half = lanes >> 1
    return [jnp.take_along_axis(v, half, axis=1), jnp.take_along_axis(v, half + 64, axis=1)]


def act_and_slope(z):
    t = jnp.tanh(0.5 * z)
    a = 0.65 + 0.35 * t
    return z * a, a + (0.175 * z) * (1.0 - t * t)


def kernel(
    sizes, vol, w1_hbm, w2_hbm, cot, out_act, out_pg, out_s1, out_s2,
    vbuf, vf, u1, slope, pb, ph, u2, cotb, ch, cotf, actf, db, fd, u3, bkf,
    w1, w2, a1s, a2s, w2f, a1, a2, a2h, a3, acc1, acc2, pack2, p1, q1, r1, r2, res,
    local_sem, halo_send, halo_recv, sum_send, sum_recv,
):
    (nx, nzh, ny), nb = sizes
    n_space = nx * nzh * ny
    g1 = nx * ny
    tp = 16 // g1
    sp, bt = lax.axis_index("space"), lax.axis_index("batch")
    xi = lax.div(sp, nzh * ny)
    zi = lax.rem(lax.div(sp, ny), nzh)
    yi = lax.rem(sp, ny)
    i1 = xi * ny + yi
    core = lax.rem(bt, 2)
    nzl = nb // 2
    nz = nzh * nzl
    iz = zi * nzl + lax.div(bt, 2)
    right = lax.rem(sp + 1, n_space)
    left = lax.rem(sp + n_space - 1, n_space)

    def at(step):
        dx, dy, dz, dc = step
        x, y, z, c = lax.rem(xi + dx, nx), lax.rem(yi + dy, ny), lax.rem(iz + dz, nz), lax.rem(core + dc, 2)
        place = (x * (nzh * ny) + lax.div(z, nzl) * ny + y, lax.rem(z, nzl) * 2 + c)
        return place, x * ny + y, c

    slab_group = offsets(nx, ny, 1, 1)
    column = offsets(1, 1, nz, 2)

    barrier = pltpu.get_barrier_semaphore()
    for side in (left, right):
        pl.semaphore_signal(barrier, inc=1, device_id=(side, bt), device_id_type=MESH)

    others = slab_group + column
    near = lambda d: hops(d[0], nx) + hops(d[1], ny) + hops(d[2], nz) + 0.1 * d[3]
    for step in sorted(others, key=near, reverse=True):
        pl.semaphore_signal(barrier, inc=1, device_id=at(step)[0], device_id_type=MESH)

    own = []
    for s in range(2):
        for x in range(4):
            own.append(pltpu.make_async_copy(vol.at[s, :, x], vbuf.at[s, x + 1], local_sem.at[s * 4 + x]))
    for s in range(2):
        for x in range(2):
            own.append(pltpu.make_async_copy(cot.at[s, :, x], cotb.at[s, x], local_sem.at[8 + s * 2 + x]))
    own.append(pltpu.make_async_copy(w1_hbm, w1, local_sem.at[12]))
    own.append(pltpu.make_async_copy(w2_hbm, w2, local_sem.at[13]))
    for c in own:
        c.start()
    for c in own[0:8]:
        c.wait()

    pl.semaphore_wait(barrier, 2 + len(others))

    def both_ways(k, to_right, land_right, to_left, land_left):
        one = pltpu.make_async_remote_copy(
            src_ref=to_right, dst_ref=land_right, send_sem=halo_send.at[k, 0], recv_sem=halo_recv.at[k, 0],
            device_id=(right, bt), device_id_type=MESH,
        )
        two = pltpu.make_async_remote_copy(
            src_ref=to_left, dst_ref=land_left, send_sem=halo_send.at[k, 1], recv_sem=halo_recv.at[k, 1],
            device_id=(left, bt), device_id_type=MESH,
        )
        return one, two

    halos = [both_ways(s, vbuf.at[s, 4], vbuf.at[s, 0], vbuf.at[s, 1], vbuf.at[s, 5]) for s in range(2)]
    for pair in halos:
        for c in pair:
            c.start()
    for c in own[8:]:
        c.wait()
    cot_pairs = [both_ways(6 + s, cotb.at[s, 1], ch.at[s, 0], cotb.at[s, 0], ch.at[s, 1]) for s in range(2)]

    def arrive(pair, low, high):
        for c in pair:
            c.wait_recv()

        @pl.when(sp == 0)
        def _():
            low[...] = jnp.zeros_like(low)

        @pl.when(sp == n_space - 1)
        def _():
            high[...] = jnp.zeros_like(high)

    a1s[...] = jnp.zeros_like(a1s)
    for kx in range(3):
        for ky in range(3):
            for kz in range(3):
                row = ky * 80 + kz * 24 + kx * 4
                a1s[row : row + 4, 0:16] = w1[kx, ky, kz].astype(F32)
    base = a1s[...]
    t1 = base
    for x in range(1, 4):
        t1 = t1 + pltpu.roll(pltpu.roll(base, 4 * x, 0), 16 * x, 1)
    a1[...] = t1.T[0:64].astype(BF16)

    w2f[...] = jnp.zeros_like(w2f)
    w2f[:, 0:32] = w2[...].reshape(432, 32).astype(F32)
    a2s[...] = jnp.zeros_like(a2s)
    for ky in range(3):
        for kx in range(3):
            a2s[ky, kx * 48 : kx * 48 + 48, :] = w2f[(kx * 3 + ky) * 48 : (kx * 3 + ky) * 48 + 48, :]
        base = a2s[ky]
        both = (base + pltpu.roll(pltpu.roll(base, 48, 0), 32, 1)).T[0:64, 0:192].astype(BF16)
        a2[64 * ky : 64 * ky + 64, :] = both
        for x in range(2):
            a2h[x, 32 * ky : 32 * ky + 32, :] = both[32 * x : 32 * x + 32]
    for ky in range(3):
        for kz in range(3):
            rows = [((kx * 3 + 2 - ky) * 3 + 2 - kz) * 16 for kx in range(3)]
            blocks = [w2f[r : r + 16, :] for r in rows]
            first = blocks[2] + pltpu.roll(blocks[1], 32, 1) + pltpu.roll(blocks[0], 64, 1)
            both = jnp.concatenate([first, pltpu.roll(first, 32, 1)], axis=0)
            a3[32 * ky : 32 * ky + 32, kz * 128 : kz * 128 + 128] = both.astype(BF16)

    for s in range(2):
        u1[s, 0:80, :] = jnp.zeros((80, 256), BF16)
        u1[s, 1360:1456, :] = jnp.zeros((96, 256), BF16)
        for y in (0, 9):
            db[s, y] = jnp.zeros((64, 128), BF16)
        for y in (0, 17):
            fd[s, y] = jnp.zeros((64, 256), BF16)

    def sent_off(*pairs):
        for pair in pairs:
            for c in pair:
                c.wait_send()

    sent_off(*halos)
    for c in (*cot_pairs[0], *cot_pairs[1]):
        c.start()

    def stage1(s):
        arrive(halos[s], vbuf.at[s, 0], vbuf.at[s, 5])
        planes = vbuf[s].reshape(384, 256).astype(F32)
        for half in range(2):
            vf[half, 0:384] = planes[:, 128 * half : 128 * half + 128]
        for y in range(16):
            v = jnp.concatenate([vf[half, pl.ds(y, 24, stride=16), :] for half in range(2)], axis=1)
            before, after = shifts(v)
            rows = jnp.concatenate([before, v, after, jnp.zeros((8, 256), F32)], axis=0)
            u1[s, (y + 1) * 80 : (y + 2) * 80, :] = rows.astype(BF16)
        for j in range(8):
            total = None
            for i in range(2):
                y = 2 * j + i
                pre = dot(a1[...], u1[s, y * 80 : y * 80 + 256, :])
                act, sl = act_and_slope(pre)
                slope[s, y * 64 : y * 64 + 64, :] = 0.125 * sl
                total = act if total is None else total + act
            pairs = jnp.concatenate([total[0:16] + total[16:32], total[32:48] + total[48:64]], axis=0)
            pooled = (0.125 * pair_sums(pairs)).astype(BF16)
            for x in range(2):
                pb[s, x, j] = pooled[16 * x : 16 * x + 16]
            mid = pooled.astype(F32)
            before, after = shifts(mid)
            for x in range(2):
                part = slice(16 * x, 16 * x + 16)
                rows = jnp.concatenate([before[part], mid[part], after[part]], axis=0)
                at = j * 288 + (x + 2) * 48
                u2[s, at : at + 48, :] = rows.astype(BF16)
        near = both_ways(2 + s, pb.at[s, 1], ph.at[s, 0, 1], pb.at[s, 0], ph.at[s, 1, 0])
        far = both_ways(4 + s, pb.at[s, 0], ph.at[s, 0, 0], pb.at[s, 1], ph.at[s, 1, 1])
        for c in near:
            c.start()
        return near, far

    def fill(s, planes):
        for j in range(8):
            mid = jnp.concatenate([ph[s, side, x, j] for side, x, at in planes], axis=0).astype(F32)
            before, after = shifts(mid)
            for k, (side, x, at) in enumerate(planes):
                part = slice(16 * k, 16 * k + 16)
                rows = jnp.concatenate([before[part], mid[part], after[part]], axis=0)
                u2[s, j * 288 + at * 48 : j * 288 + at * 48 + 48, :] = rows.astype(BF16)

    def convolved(s, matrix, first, count):
        parts = []
        for j in range(4):
            both = [u2[s, (2 * j + i) * 288 + first : (2 * j + i) * 288 + first + 192, :] for i in range(2)]
            part = dot(matrix, jnp.concatenate(both, axis=1))
            parts += [part[:, 0:128], part[:, 128:256]]
        out = []
        for j in range(8):
            pre = parts[j][count : 2 * count]
            if j > 0:
                pre = pre + parts[j - 1][0:count]
            if j < 7:
                pre = pre + parts[j + 1][2 * count : 3 * count]
            out.append(pre)
        return out

    def spread_delta(s, j, delta, places):
        mid = delta.astype(F32)
        before, after = shifts(mid)
        for kz, rows in enumerate((before, mid, after)):
            rows = rows.astype(BF16)
            for first, count, at in places:
                low = j * 384 + kz * 128 + at
                u3[s, low : low + count, :] = rows[first : first + count]

    def second_own(s, near):
        for x in range(2):
            cotf[x + 1, 0:256] = cotb[s, x].reshape(256, 128).astype(F32)
        arrive(near, ph.at[s, 0, 1], ph.at[s, 1, 0])
        fill(s, ((0, 1, 1), (1, 0, 4)))
        for j, pre in enumerate(convolved(s, a2[...], 48, 64)):
            act, sl = act_and_slope(pre)
            for x in range(2):
                actf[s, pl.ds(x * 8 + j, 32, stride=16), :] = act[32 * x : 32 * x + 32]
            got = [cotf[1 + x, pl.ds(j, 32, stride=8), :] for x in range(2)]
            db[s, j + 1] = (jnp.concatenate(got, axis=0) * sl).astype(BF16)

    def after_own(s):
        out_act[s] = actf[s, 0:512].reshape(32, 2, 8, 128).astype(BF16)
        for j in range(8):
            spread_delta(s, j, db[s, j + 1], ((0, 64, 32),))

    def second_beside(s, far):
        arrive(cot_pairs[s], ch.at[s, 0], ch.at[s, 1])
        for side in range(2):
            cotf[3 * side, 0:256] = ch[s, side].reshape(256, 128).astype(F32)
        arrive(far, ph.at[s, 0, 0], ph.at[s, 1, 1])
        fill(s, ((0, 0, 0), (1, 1, 5)))
        low = convolved(s, a2h[0], 0, 32)
        high = convolved(s, a2h[1], 96, 32)
        for j in range(8):
            sl = act_and_slope(jnp.concatenate([low[j], high[j]], axis=0))[1]
            got = [cotf[3 * side, pl.ds(j, 32, stride=8), :] for side in range(2)]
            delta = (jnp.concatenate(got, axis=0) * sl).astype(BF16)
            spread_delta(s, j, delta, ((0, 32, 0), (32, 32, 96)))

    def second_grad(s):
        fields = [u2[s, y * 288 + 48 : y * 288 + 240, :] for y in range(8)]
        deltas = [db[s, y : y + 3].reshape(192, 128) for y in range(8)]
        return dot_nt(jnp.concatenate(fields, axis=1), jnp.concatenate(deltas, axis=1))

    def stage3(s):
        parts = []
        for j in range(4):
            both = jnp.concatenate([u3[s, (2 * j + i) * 384 : (2 * j + i) * 384 + 384, :] for i in range(2)], axis=1)
            part = dot(a3[...], both)
            parts += [part[:, 0:128], part[:, 128:256]]
        for j in range(8):
            back = parts[j][32:64]
            if j > 0:
                back = back + parts[j - 1][0:32]
            if j < 7:
                back = back + parts[j + 1][64:96]
            for x in range(2):
                bkf[pl.ds(x * 8 + j, 16, stride=16), :] = back[16 * x : 16 * x + 16]
            up = jnp.concatenate(doubled(back), axis=1)
            up = jnp.concatenate([up[0:16], up[0:16], up[16:32], up[16:32]], axis=0)
            for y in (2 * j, 2 * j + 1):
                fd[s, y + 1] = (up * slope[s, y * 64 : y * 64 + 64, :]).astype(BF16)
        out_pg[s] = bkf[0:256].reshape(16, 2, 8, 128).astype(BF16)

    def first_grad(s):
        total = None
        for k in range(4):
            ys = range(4 * k, 4 * k + 4)
            fields = [u1[s, (y + 1) * 80 : (y + 2) * 80, :] for y in ys]
            deltas = [fd[s, y : y + 3].reshape(192, 256) for y in ys]
            part = dot_nt(jnp.concatenate(deltas, axis=1), jnp.concatenate(fields, axis=1))
            total = part if total is None else total + part
        return total

    def exchange(phase, group, src, dst):
        sent = []
        for k, step in enumerate(group):
            place, slab, c = at(step)
            copy = pltpu.make_async_remote_copy(
                src_ref=src(slab, c), dst_ref=dst, send_sem=sum_send.at[phase, k], recv_sem=sum_recv.at[phase, k],
                device_id=place, device_id_type=MESH,
            )
            copy.start()
            sent.append(copy)

        def finished():
            for copy in sent:
                copy.wait()

        return finished

    halves = [stage1(0), stage1(1)]
    for c in (*halves[0][1], *halves[1][1]):
        c.start()
    second_own(0, halves[0][0])
    acc2[:, 0:192] = second_grad(0)
    after_own(0)
    second_own(1, halves[1][0])
    acc2[:, 0:192] += second_grad(1)

    lanes = lax.broadcasted_iota(jnp.int32, (144, 128), 1)
    f2 = None
    for f in range(3):
        ky = 2 - f
        tile = acc2[:, 128 * (f // 2) : 128 * (f // 2) + 128]
        move = 32 * ky - 64 * (f % 2)
        part = pltpu.roll(tile[0:144], move % 128, 1) if move % 128 else tile[0:144]
        part = part + pltpu.roll(tile[48:192], (move - 32) % 128, 1)
        part = jnp.where((lanes >= 32 * ky) & (lanes < 32 * ky + 32), part, 0.0)
        f2 = part if f2 is None else f2 + part
    rest = []
    for ky in range(3):
        part = pltpu.roll(f2[128:144], 96 - 32 * ky, 1)
        rest.append(jnp.where(lanes[0:16] >= 96, part, 0.0))
    rest = jnp.concatenate(rest + [jnp.zeros((80, 128), F32)], axis=0)
    pack2[...] = (f2[0:128] + rest).reshape(16, 8, 128)

    r1[i1] = pack2[pl.ds(i1 * tp, tp)]
    scattered = exchange(0, slab_group, lambda slab, c: pack2.at[pl.ds(slab * tp, tp)], r1.at[i1])

    acc1[...] = jnp.zeros_like(acc1)
    after_own(1)
    for s in range(2):
        second_beside(s, halves[s][1])
        stage3(s)
        acc1[0:192, 0:80] += first_grad(s)

    rows = lax.broadcasted_iota(jnp.int32, (80, 128), 0)
    lanes = lax.broadcasted_iota(jnp.int32, (80, 128), 1)
    folded = []
    turned = acc1[...].T[0:80]
    for half in range(2):
        g = turned[:, 128 * half : 128 * half + 128]
        f1 = g
        for x in range(1, 4):
            f1 = f1 + pltpu.roll(pltpu.roll(g, 80 - 4 * x, 0), 128 - 16 * x, 1)
        f1 = jnp.where((lanes & 63) < 16, f1, 0.0)
        f1c = None
        for kz in range(3):
            part = jnp.where((rows >= 24 * kz) & (rows < 24 * kz + 12), f1, 0.0)
            part = pltpu.roll(part, 80 - 12 * kz, 0) if kz else part
            f1c = part if f1c is None else f1c + part
        folded.append(f1c[0:40])
    packed = [None, None]
    for f in range(3):
        for r in range(5):
            k = f * 5 + r
            part = folded[f // 2][8 * r : 8 * r + 8]
            part = jnp.where((lanes[0:8] >> 6) == f % 2, part, 0.0)
            move = (16 * (k // 2) - 64 * (f % 2)) % 128
            part = pltpu.roll(part, move, 1) if move else part
            packed[k % 2] = part if packed[k % 2] is None else packed[k % 2] + part
    packed = jnp.concatenate(packed, axis=0)
    p1[i1] = packed
    within = exchange(3, slab_group, lambda slab, c: p1.at[i1], p1.at[i1])
    scattered()
    r2[iz * 2 + core] = jnp.sum(r1[...], axis=0)
    crossed = exchange(1, column, lambda slab, c: r2.at[iz * 2 + core], r2.at[iz * 2 + core])
    within()
    q1[iz * 2 + core] = jnp.sum(p1[...], axis=0)
    over = exchange(4, column, lambda slab, c: q1.at[iz * 2 + core], q1.at[iz * 2 + core])
    crossed()
    res[i1] = jnp.sum(r2[...], axis=0)
    gathered = exchange(2, slab_group, lambda slab, c: res.at[i1], res.at[i1])
    over()
    out_s1[...] = jnp.sum(q1[...], axis=0)
    gathered()
    sent_off(*(h[0] for h in halves), *(h[1] for h in halves), *cot_pairs)
    out_s2[...] = res[...].reshape(128, 128)


def finish(scales, act, pg, sums1, sums2, out_act, out_pg, out_g1, out_g2, flat, g1v, g2v, sem):
    stores = [
        pltpu.make_async_copy(src, dst, sem.at[k])
        for k, (src, dst) in enumerate(((act, out_act), (pg, out_pg), (g2v, out_g2), (g1v, out_g1)))
    ]
    for c in stores[0:2]:
        c.start()
    total = sums2[...] * scales[1]
    rest = pltpu.roll(total[0:48], 32, 1)
    for ky in range(3):
        part = pltpu.roll(total, 128 - 32 * ky, 1) if ky else total
        whole = jnp.concatenate([part, rest[ky * 16 : ky * 16 + 16]], axis=0)[:, 0:32]
        for kx in range(3):
            g2v[kx, ky] = whole[kx * 48 : kx * 48 + 48].reshape(3, 16, 32)
    stores[2].start()
    total = sums1[...] * scales[0]
    for k in range(15):
        part = total[8 * (k % 2) : 8 * (k % 2) + 8]
        flat[8 * k : 8 * k + 8, :] = pltpu.roll(part, 128 - 16 * (k // 2), 1) if k > 1 else part
    for kx in range(3):
        for ky in range(3):
            for kz in range(3):
                row = (2 - ky) * 40 + kz * 12 + kx * 4
                g1v[kx, ky, kz] = flat[row : row + 4, 0:16]
    stores[3].start()
    for c in stores:
        c.wait()


def solution(mesh):
    sizes = (space_grid(mesh.shape["space"]), mesh.shape["batch"])

    def body(volumes, first_kernel, second_kernel, cotangent):
        cells = math.prod(volumes.shape) // volumes.shape[1] * mesh.size
        scales = (1.0 / math.sqrt(cells), 1.0 / math.sqrt(cells / 8))
        w1 = jnp.transpose(first_kernel, (2, 3, 4, 1, 0))
        w2 = jnp.transpose(second_kernel, (2, 3, 4, 1, 0))
        hbm = pl.BlockSpec(memory_space=pltpu.HBM)
        vmem = pl.BlockSpec(memory_space=pltpu.VMEM)
        g1 = sizes[0][0] * sizes[0][2]
        g2 = sizes[0][1] * sizes[1]
        vmem_limit = 63 * 1024 * 1024
        act, pooled_grad, sums1, sums2 = pl.pallas_call(
            functools.partial(kernel, sizes),
            out_shape=(
                pltpu.VMEM((2, 32, 2, 8, 128), BF16),
                pltpu.VMEM((2, 16, 2, 8, 128), BF16),
                pltpu.VMEM((16, 128), F32),
                pltpu.VMEM((128, 128), F32),
            ),
            in_specs=[hbm] * 4,
            out_specs=(vmem,) * 4,
            scratch_shapes=[
                pltpu.VMEM((2, 6, 4, 16, 256), BF16),
                pltpu.VMEM((2, 400, 128), F32),
                pltpu.VMEM((2, 1456, 256), BF16),
                pltpu.VMEM((2, 1024, 256), F32),
                pltpu.VMEM((2, 2, 8, 16, 128), BF16),
                pltpu.VMEM((2, 2, 2, 8, 16, 128), BF16),
                pltpu.VMEM((2, 2304, 128), BF16),
                pltpu.VMEM((2, 2, 32, 8, 128), BF16),
                pltpu.VMEM((2, 2, 32, 8, 128), BF16),
                pltpu.VMEM((4, 264, 128), F32),
                pltpu.VMEM((2, 528, 128), F32),
                pltpu.VMEM((2, 10, 64, 128), BF16),
                pltpu.VMEM((2, 18, 64, 256), BF16),
                pltpu.VMEM((2, 3072, 128), BF16),
                pltpu.VMEM((272, 128), F32),
                pltpu.VMEM((3, 3, 3, 4, 16), BF16),
                pltpu.VMEM((3, 3, 3, 16, 32), BF16),
                pltpu.VMEM((256, 128), F32),
                pltpu.VMEM((3, 256, 128), F32),
                pltpu.VMEM((432, 128), F32),
                pltpu.VMEM((64, 256), BF16),
                pltpu.VMEM((192, 192), BF16),
                pltpu.VMEM((2, 96, 192), BF16),
                pltpu.VMEM((96, 384), BF16),
                pltpu.VMEM((256, 128), F32),
                pltpu.VMEM((192, 256), F32),
                pltpu.VMEM((16, 8, 128), F32),
                pltpu.VMEM((g1, 16, 128), F32),
                pltpu.VMEM((g2, 16, 128), F32),
                pltpu.VMEM((g1, 16 // g1, 8, 128), F32),
                pltpu.VMEM((g2, 16 // g1, 8, 128), F32),
                pltpu.VMEM((g1, 16 // g1, 8, 128), F32),
                pltpu.SemaphoreType.DMA((14,)),
                pltpu.SemaphoreType.DMA((8, 2)),
                pltpu.SemaphoreType.DMA((8, 2)),
                pltpu.SemaphoreType.DMA((5, max(g1, g2))),
                pltpu.SemaphoreType.DMA((5, max(g1, g2))),
            ],
            compiler_params=pltpu.CompilerParams(
                collective_id=0, has_side_effects=True, vmem_limit_bytes=vmem_limit
            ),
        )(volumes, w1, w2, cotangent)
        act, pooled_grad, grad1, grad2 = pl.pallas_call(
            functools.partial(finish, scales),
            out_shape=(
                jax.ShapeDtypeStruct((2, 32, 2, 8, 128), BF16),
                jax.ShapeDtypeStruct((2, 16, 2, 8, 128), BF16),
                jax.ShapeDtypeStruct((3, 3, 3, 4, 16), F32),
                jax.ShapeDtypeStruct((3, 3, 3, 16, 32), F32),
            ),
            in_specs=[vmem] * 4,
            out_specs=(hbm,) * 4,
            scratch_shapes=[
                pltpu.VMEM((128, 128), F32),
                pltpu.VMEM((3, 3, 3, 4, 16), F32),
                pltpu.VMEM((3, 3, 3, 16, 32), F32),
                pltpu.SemaphoreType.DMA((4,)),
            ],
            compiler_params=pltpu.CompilerParams(vmem_limit_bytes=16 * 1024 * 1024),
        )(act, pooled_grad, sums1, sums2)
        return (
            act,
            pooled_grad,
            jnp.transpose(grad1, (4, 3, 0, 1, 2)),
            jnp.transpose(grad2, (4, 3, 0, 1, 2)),
        )

    return jax.shard_map(
        body,
        mesh=mesh,
        in_specs=(
            P("batch", None, "space", None, None),
            P(),
            P(),
            P("batch", None, "space", None, None),
        ),
        out_specs=(
            P("batch", None, "space", None, None),
            P("batch", None, "space", None, None),
            P(),
            P(),
        ),
        check_vma=False,
    )
```
